512 devices in a mesh: rows: 256 (over y, z, x), rep: 2 (over core).
Axes of the slice: x: 4, y: 8, z: 8, core: 2. Of those that a mesh axis runs over, the one named last changes fastest.
Arguments:
- hamiltonian: bfloat16 [1024, 8, 128, 128], P('rows'), may hold values from -6 to 6
- x_correction: bfloat16 [1024, 8, 128, 128], P('rows'), may hold values from -0.3125 to 0.3125
- block_cols: int32 [1024, 8], P('rows'), may hold values from 0 to 1023, as said below
- block_mask: int32 [1024, 8], P('rows'), may hold values from 0 to 1, as said below
Outputs:
- density: bfloat16 [1024, 8, 128, 128], P('rows', 'rep')
The draws below stay inside these ranges and needn't reach their ends.
Inputs may be any that keep to these rules, and one draw needn't show every extreme that they name: `block_cols`: in row i the slots with block_mask 1 name distinct block columns at most 4 away from i; slot 0 names i itself. Padding slots hold a column clipped into range. `block_mask`: slot 0 of every row is 1.
All inputs are finite; a program needn't handle non-finite values.
Results may differ from the reference program's by a relative error of at most 0.038.
Values may be sent and summed in bfloat16 or wider, within the bound.
No kernel may reach another device: no remote copies, remote signals or barrier semaphores. Data moves between devices by JAX's collectives and lax.ppermute only.
A program may use at most 64 MiB of HBM per device.

```python
import math
import jax
import jax.numpy as jnp
from jax import lax

B = 128
K = 8
BAND = 4
STEPS = 2
NB = 1024


def pattern(key):
    span = 2 * BAND + 1
    scores = jax.random.randint(key, (NB, span), 0, 1 << 20) * span + jnp.arange(span, dtype=jnp.int32)
    scores = scores.at[:, BAND].set(jnp.int32(1 << 30))
    unused, picked = lax.top_k(scores, K)
    offsets = picked.astype(jnp.int32) - BAND
    target = jnp.arange(NB, dtype=jnp.int32)[:, None] + offsets
    inside = (target >= 0) & (target < NB)
    keep = (jax.random.randint(jax.random.fold_in(key, 11), (NB, K), 0, 4) > 0) | (offsets == 0)
    return (jnp.clip(target, 0, NB - 1).astype(jnp.int32), (inside & keep).astype(jnp.int32))


def draw_block_cols(key, part):
    columns, marks = pattern(key)
    return columns


def draw_block_mask(key, part):
    columns, marks = pattern(key)
    return marks


def steps_of(key, dims, pieces, smallest, largest):
    level = 1.0
    for position, parts in pieces:
        draws = jax.random.uniform(jax.random.fold_in(jax.random.fold_in(key, 6), position), (parts,), jnp.float32, smallest / len(pieces), largest / len(pieces))
        level = level * jnp.repeat(jnp.exp(draws), dims[position] // parts).reshape((-1,) + (1,) * (len(dims) - 1 - position))
    return level


def centred(rng, extent, deviation, reach, pieces=(), kind=jnp.bfloat16):
    entries = jax.random.normal(rng, extent, jnp.float32) * deviation
    if len(pieces) > 0:
        entries = steps_of(rng, extent, pieces, -0.22, 0.18) * entries
    return jnp.clip(entries, min=-reach, max=reach).astype(kind)


def setup_inputs(seed: int = 0) -> dict:
    seeds = jax.random.split(jax.random.key(seed), 5)
    return {
        "hamiltonian": centred(seeds[0], (NB, K, B, B), 1.0, 6.0, ((0, 256),)),
        "x_correction": centred(seeds[1], (NB, K, B, B), 0.02, 0.3125, ((0, 256),)),
        "block_cols": draw_block_cols(jax.random.fold_in(seeds[4], 71), 0),
        "block_mask": draw_block_mask(jax.random.fold_in(seeds[4], 71), 0),
    }


def product(left, right, block_cols, block_mask):
    count, slots = block_cols.shape
    size = left.shape[-1]
    flat_right = right.reshape(count * slots, size, size)
    right_cols = block_cols[block_cols]
    right_mask = block_mask[block_cols]
    order = jnp.arange(slots, dtype=jnp.int32)

    def one_row(items):
        left_row, col_row, mask_row, cols_there, mask_there = items
        match = (cols_there[None, :, :] == col_row[:, None, None]) & (mask_there[None, :, :] == 1) & (mask_row[None, :, None] == 1)
        slot_there = lax.optimization_barrier(jnp.sum(jnp.where(match, order, 0), axis=-1))
        found = jnp.any(match, axis=-1)
        picked = flat_right[col_row[None, :] * slots + slot_there]
        picked = jnp.where(found[:, :, None, None], picked.astype(jnp.float32), jnp.float32(0.0))
        summed = jnp.einsum('tab,stbc->sac', left_row.astype(jnp.float32), picked)
        return (summed * mask_row.astype(jnp.float32)[:, None, None]).astype(jnp.bfloat16)
    return lax.map(one_row, (left, block_cols, block_mask, right_cols, right_mask), batch_size=16)

def reference(hamiltonian, x_correction, block_cols, block_mask):
    count, slots = block_cols.shape
    size = hamiltonian.shape[-1]
    identity = jnp.eye(size, dtype=jnp.float32)
    on_diag = (block_cols == jnp.arange(count, dtype=jnp.int32)[:, None]).astype(jnp.float32)[:, :, None, None]
    xmat = (identity * on_diag + x_correction.astype(jnp.float32)).astype(jnp.bfloat16)
    half_product = product(xmat, hamiltonian, block_cols, block_mask)
    orthogonal = product(half_product, xmat, block_cols, block_mask)
    factor = 0.6 / math.sqrt(slots * size)
    density = (0.5 * identity * on_diag - factor * orthogonal.astype(jnp.float32)).astype(jnp.bfloat16)
    for step in range(STEPS):
        square = product(density, density, block_cols, block_mask)
        cube = product(square, density, block_cols, block_mask)
        density = (3.0 * square.astype(jnp.float32) - 2.0 * cube.astype(jnp.float32)).astype(jnp.bfloat16)
    return density
```

```python
import math

import jax
import jax.numpy as jnp
from jax import lax
from jax.experimental import pallas as pl
from jax.experimental.pallas import tpu as pltpu
from jax.sharding import PartitionSpec as P

BAND = 4
STEPS = 2
S = 128
Q = 4 * S
H = 2 * S
TRI = [(p, m) for p in range(4) for m in range(p, 4)]
BF = jnp.bfloat16
F32 = jnp.float32
LEFT, OWN, RIGHT = (0, 1), (2, 3), (4, 5)

VMEM = pl.BlockSpec(memory_space=pltpu.VMEM)
SMEM = pl.BlockSpec(memory_space=pltpu.SMEM)
SQUARE = jax.ShapeDtypeStruct((Q, Q), BF)
CORNER = jax.ShapeDtypeStruct((len(TRI), S, S), BF)
BANDED = jax.ShapeDtypeStruct((Q, 3 * Q), BF)


def call(kernel, outs, out_specs, in_specs, scratch, flops, *args):
    return pl.pallas_call(
        kernel,
        out_shape=outs,
        in_specs=in_specs,
        out_specs=out_specs,
        scratch_shapes=scratch,
        compiler_params=pltpu.CompilerParams(vmem_limit_bytes=24 * 1024 * 1024),
        cost_estimate=pl.CostEstimate(flops=flops, bytes_accessed=4 << 20, transcendentals=0),
    )(*args)


def place(cols_ref, mask_ref, a, s):
    first = lax.axis_index("rows") * 4 - BAND
    core = lax.axis_index("rep")
    k = cols_ref[a, s] - first
    k = jnp.clip(k, 0, 11)
    k = jnp.where(core == 1, 11 - k, k)
    row = jnp.where(core == 1, 3 - a, a)
    t = jnp.where(k < 4, 3 - k, k)
    return mask_ref[a, s] == 1, row, t


def at(index):
    return pl.ds(pl.multiple_of(index * S, S), S)


def corner_index(p, m):
    return ((p * (7 - p)) >> 1) + m


def eye():
    rows = lax.broadcasted_iota(jnp.int32, (S, S), 0)
    cols = lax.broadcasted_iota(jnp.int32, (S, S), 1)
    return (rows == cols).astype(F32)


def send_slots(cols_ref, mask_ref, block_of, a_ref, b_ref):
    a_ref[...] = jnp.zeros_like(a_ref)
    b_ref[...] = jnp.zeros_like(b_ref)
    for a in range(4):
        for s in range(8):
            active, row, t = place(cols_ref, mask_ref, a, s)

            @pl.when(active & (t >= 4) & (t < 8))
            def _():
                b_ref[at(3 - row), at(jnp.clip(7 - t, 0, 3))] = block_of(a, s)

            @pl.when(active & (t >= 8))
            def _():
                index = corner_index(3 - row, 11 - t)
                a_ref[jnp.clip(index, 0, 9)] = block_of(a, s)


def pack_h(cols_ref, mask_ref, h_ref, a_ref, b_ref):
    send_slots(cols_ref, mask_ref, lambda a, s: h_ref[a, s], a_ref, b_ref)


def pack_x(cols_ref, mask_ref, h_ref, x_ref, xa_ref, xb_ref, ho_ref, xo_ref, table_ref):
    diag = eye()

    def x_block(a, s):
        if s == 0:
            return (x_ref[a, s].astype(F32) + diag).astype(BF)
        return x_ref[a, s]

    send_slots(cols_ref, mask_ref, x_block, xa_ref, xb_ref)
    ho_ref[...] = jnp.zeros_like(ho_ref)
    xo_ref[...] = jnp.zeros_like(xo_ref)
    for a in range(4):
        for t in range(12):
            table_ref[a, t] = 0
    for a in range(4):
        for s in range(8):
            active, row, t = place(cols_ref, mask_ref, a, s)

            @pl.when(active)
            def _():
                ho_ref[at(row), at(t)] = h_ref[a, s]
                xo_ref[at(row), at(t)] = x_block(a, s)
                table_ref[row, t] = 1


def spread_mine(corner_ref, square_ref):
    square_ref[H:, :H] = jnp.zeros((H, H), BF)
    square_ref[S : 2 * S, :S] = jnp.zeros((S, S), BF)
    square_ref[3 * S :, H : 3 * S] = jnp.zeros((S, S), BF)
    for index, (p, m) in enumerate(TRI):
        square_ref[p * S : (p + 1) * S, m * S : (m + 1) * S] = corner_ref[index]


def spread_twin(corner_ref, square_ref):
    square_ref[H:, H:] = jnp.zeros((H, H), BF)
    square_ref[S : 2 * S, 3 * S :] = jnp.zeros((S, S), BF)
    square_ref[3 * S :, S:H] = jnp.zeros((S, S), BF)
    for index, (p, m) in enumerate(TRI):
        square_ref[p * S : (p + 1) * S, (3 - m) * S : (4 - m) * S] = corner_ref[index]


def tile(ref, i, j):
    return ref[i * H : (i + 1) * H, j * H : (j + 1) * H]


def right_operand(ll, lc, own, rc, rr):
    def get(t, u):
        if t in OWN:
            if (t, u) in ((3, 1), (2, 5)):
                return None
            return own(t - 2, u)
        if t in LEFT:
            if u in LEFT:
                return tile(ll, t, u)
            if u in OWN and (t, u) != (1, 3):
                return tile(lc, t, u - 2)
            return None
        if u in RIGHT:
            return tile(rr, t - 4, u - 4)
        if u in OWN and (t, u) != (5, 2):
            return tile(rc, t - 4, u - 2)
        return None

    return get


def left_tile(ref, r, t):
    if (r, t) in ((1, 1), (0, 5)):
        return None
    return tile(ref, r, t)


def product(left, right, columns, finish):
    for u in columns:
        for r in range(2):
            if (r, u) in ((1, 1), (0, 5)):
                continue
            total = None
            for t in range(6):
                x = left(r, t)
                y = right(t, u)
                if x is None or y is None:
                    continue
                term = jnp.dot(x, y, preferred_element_type=F32)
                total = term if total is None else total + term
            finish(r, u, total)


def each_block(table_ref, r, u, total, store):
    for i in range(2):
        for j in range(2):
            row, t = 2 * r + i, 2 * u + j
            block = total[i * S : (i + 1) * S, j * S : (j + 1) * S]
            block = jnp.where(table_ref[row, t] == 1, block, 0.0)
            store(row, t, block)


def put(ref, row, t, block):
    ref[row * S : (row + 1) * S, t * S : (t + 1) * S] = block


def put_square(ref, send_ref, row, t, block):
    put(ref, row, t - 4, block)
    put(send_ref, 3 - row, 7 - t, block)


def put_corner(ref, send_ref, row, t, block):
    put(ref, row, t - 8, block)
    p, m = 3 - row, 11 - t
    if m >= p:
        send_ref[TRI.index((p, m))] = block


def half_kernel(factor, table, xo, ho, hb, ha, hb2, ha2, xa, xa2, half_ref, pc_ref, sb_ref, lc, rc, xlc, xrc):
    spread_mine(ha, rc)
    spread_twin(ha2, lc)
    spread_mine(xa, xrc)
    spread_twin(xa2, xlc)
    half_ref[H:, H:Q] = jnp.zeros((H, H), BF)
    half_ref[:H, 2 * Q + H :] = jnp.zeros((H, H), BF)
    right = right_operand(hb2, lc, lambda r, u: tile(ho, r, u), rc, hb)

    def keep(r, u, total):
        each_block(table, r, u, total, lambda row, t, b: put(half_ref, row, t, b.astype(BF)))

    product(lambda r, t: left_tile(xo, r, t), right, range(6), keep)
    right = right_operand(None, xlc, lambda r, u: tile(xo, r, u), xrc, None)
    diag = eye()

    def start(r, u, total):
        def store(row, t, block):
            value = -factor * block
            if t - 4 == row:
                value = value + 0.5 * diag
            put_square(pc_ref, sb_ref, row, t, value.astype(BF))

        each_block(table, r, u, total, store)

    product(lambda r, t: left_tile(half_ref, r, t), right, OWN, start)


def side_kernel(factor, table, half, xo, xb, pr_ref, sa_ref):
    pr_ref[:H, H:] = jnp.zeros((H, H), BF)
    right = right_operand(None, None, lambda r, u: tile(xo, r, u), None, xb)

    def start(r, u, total):
        each_block(
            table,
            r,
            u,
            total,
            lambda row, t, b: put_corner(pr_ref, sa_ref, row, t, (-factor * b).astype(BF)),
        )

    product(lambda r, t: left_tile(half, r, t), right, RIGHT, start)


def squares(table, pc, pr, sa2, hb, ha, hb2, ha2, band, sq, lc, rc):
    spread_mine(ha, rc)
    spread_twin(ha2, lc)
    spread_twin(sa2, band.at[:, :Q])
    band[:, Q : 2 * Q] = pc[...]
    band[:, 2 * Q :] = pr[...]
    right = right_operand(hb2, lc, lambda r, u: tile(band, r, u), rc, hb)

    def keep(r, u, total):
        each_block(table, r, u, total, lambda row, t, b: put(sq, row, t, b.astype(BF)))

    product(lambda r, t: left_tile(band, r, t), right, range(6), keep)
    return right


def blocks_of(sq, row, t):
    return sq[row * S : (row + 1) * S, t * S : (t + 1) * S].astype(F32)


def step_kernel(table, pc, pr, sa2, hb, ha, hb2, ha2, nc_ref, nr_ref, sb_ref, sa_ref, band, sq, lc, rc):
    right = squares(table, pc, pr, sa2, hb, ha, hb2, ha2, band, sq, lc, rc)
    nr_ref[:H, H:] = jnp.zeros((H, H), BF)

    def step(r, u, total):
        def store(row, t, block):
            value = (3.0 * blocks_of(sq, row, t) - 2.0 * block).astype(BF)
            if u in OWN:
                put_square(nc_ref, sb_ref, row, t, value)
            else:
                put_corner(nr_ref, sa_ref, row, t, value)

        each_block(table, r, u, total, store)

    product(lambda r, t: left_tile(sq, r, t), right, RIGHT + OWN, step)


def last_kernel(cols_ref, mask_ref, table, pc, pr, sa2, hb, ha, hb2, ha2, out_ref, band, sq, lc, rc, res):
    right = squares(table, pc, pr, sa2, hb, ha, hb2, ha2, band, sq, lc, rc)

    def step(r, u, total):
        def store(row, t, block):
            put(res, row, t, (3.0 * blocks_of(sq, row, t) - 2.0 * block).astype(BF))

        each_block(table, r, u, total, store)

    product(lambda r, t: left_tile(sq, r, t), right, range(6), step)
    core = lax.axis_index("rep")
    for a in range(4):
        for s in range(4):
            active, row, t = place(cols_ref, mask_ref, a, core * 4 + s)

            @pl.when(active)
            def _():
                out_ref[a, s] = res[at(row), at(t)]

            @pl.when(jnp.logical_not(active))
            def _():
                out_ref[a, s] = jnp.zeros((S, S), BF)


def on_device(hamiltonian, x_correction, cols, mask):
    n = lax.axis_size("rows")
    factor = 0.6 / math.sqrt(cols.shape[1] * hamiltonian.shape[-1])
    outward = [(2 * i, 2 * i + 3) for i in range(n - 1)] + [(2 * i + 1, 2 * i - 2) for i in range(1, n)]

    def link(x):
        return lax.ppermute(x, ("rows", "rep"), outward)

    def swap(x):
        return lax.ppermute(x, "rep", [(0, 1), (1, 0)])

    square = pltpu.VMEM((Q, Q), BF)
    band = pltpu.VMEM((Q, 3 * Q), BF)
    sum_flops = 1 << 30

    ha, hb = call(pack_h, [CORNER, SQUARE], [VMEM] * 2, [SMEM, SMEM, VMEM], [], 0, cols, mask, hamiltonian)
    hb_in = link(hb)
    ha_in = link(ha)
    xa, xb, ho, xo, table = call(
        pack_x,
        [CORNER, SQUARE, BANDED, BANDED, jax.ShapeDtypeStruct((4, 12), jnp.int32)],
        [VMEM] * 4 + [SMEM],
        [SMEM, SMEM, VMEM, VMEM],
        [],
        0,
        cols,
        mask,
        hamiltonian,
        x_correction,
    )
    xa_in = link(xa)
    xb_in = link(xb)
    hb_twin = swap(hb_in)
    ha_twin = swap(ha_in)
    xa_twin = swap(xa_in)
    half, pc, sb = call(
        lambda *refs: half_kernel(factor, *refs),
        [BANDED, SQUARE, SQUARE],
        [VMEM] * 3,
        [SMEM] + [VMEM] * 8,
        [square] * 4,
        sum_flops,
        table, xo, ho, hb_in, ha_in, hb_twin, ha_twin, xa_in, xa_twin,
    )
    b_in = link(sb)
    pr, sa = call(
        lambda *refs: side_kernel(factor, *refs),
        [SQUARE, CORNER],
        [VMEM] * 2,
        [SMEM] + [VMEM] * 3,
        [],
        sum_flops,
        table, half, xo, xb_in,
    )
    a_in = link(sa)
    for step in range(STEPS):
        a_own = swap(sa)
        b_twin = swap(b_in)
        a_twin = swap(a_in)
        halo = (pc, pr, a_own, b_in, a_in, b_twin, a_twin)
        if step + 1 < STEPS:
            pc, pr, sb, sa = call(
                step_kernel,
                [SQUARE, SQUARE, SQUARE, CORNER],
                [VMEM] * 4,
                [SMEM] + [VMEM] * 7,
                [band, band, square, square],
                2 * sum_flops,
                table, *halo,
            )
            b_in = link(sb)
            a_in = link(sa)
        else:
            return call(
                last_kernel,
                jax.ShapeDtypeStruct((4, 4, S, S), BF),
                VMEM,
                [SMEM] * 3 + [VMEM] * 7,
                [band, band, square, square, band],
                2 * sum_flops,
                cols, mask, table, *halo,
            )


def solution(mesh):
    return jax.shard_map(
        on_device,
        mesh=mesh,
        in_specs=(
            P("rows", None, None, None),
            P("rows", None, None, None),
            P("rows", None),
            P("rows", None),
        ),
        out_specs=P("rows", "rep", None, None),
        check_vma=False,
    )
```

```python
import math

import jax
import jax.numpy as jnp
from jax import lax
from jax.experimental import pallas as pl
from jax.experimental.pallas import tpu as pltpu
from jax.sharding import PartitionSpec as P

BAND = 4
STEPS = 2
S = 128
Q = 4 * S
H = 2 * S
TRI = [(p, m) for p in range(4) for m in range(p, 4)]
BF = jnp.bfloat16
F32 = jnp.float32
LEFT, OWN, RIGHT = (0, 1), (2, 3), (4, 5)

VMEM = pl.BlockSpec(memory_space=pltpu.VMEM)
SMEM = pl.BlockSpec(memory_space=pltpu.SMEM)
SQUARE = jax.ShapeDtypeStruct((Q, Q), BF)
CORNER = jax.ShapeDtypeStruct((len(TRI), S, S), BF)
BANDED = jax.ShapeDtypeStruct((Q, 3 * Q), BF)
SEND = jax.ShapeDtypeStruct((6 * S + S // 2, Q), BF)
SUMS = jax.ShapeDtypeStruct((Q, Q), F32)
WIDE = jax.ShapeDtypeStruct((Q, 3 * Q), F32)


def call(kernel, outs, out_specs, in_specs, scratch, flops, *args, room=24):
    return pl.pallas_call(
        kernel,
        out_shape=outs,
        in_specs=in_specs,
        out_specs=out_specs,
        scratch_shapes=scratch,
        compiler_params=pltpu.CompilerParams(vmem_limit_bytes=room << 20),
        cost_estimate=pl.CostEstimate(flops=flops, bytes_accessed=4 << 20, transcendentals=0),
    )(*args)


def place(cols_ref, mask_ref, a, s):
    first = lax.axis_index("rows") * 4 - BAND
    core = lax.axis_index("rep")
    k = cols_ref[a, s] - first
    k = jnp.clip(k, 0, 11)
    k = jnp.where(core == 1, 11 - k, k)
    row = jnp.where(core == 1, 3 - a, a)
    t = jnp.where(k < 4, 3 - k, k)
    return mask_ref[a, s] == 1, row, t


def at(index):
    return pl.ds(pl.multiple_of(index * S, S), S)


def eye():
    rows = lax.broadcasted_iota(jnp.int32, (S, S), 0)
    cols = lax.broadcasted_iota(jnp.int32, (S, S), 1)
    return (rows == cols).astype(F32)


def joint_put(joint, index, block):
    if joint.shape[0] == 6 * S + S // 2 and index >= 24:
        col = (index - 24) * 2 * S
        joint[6 * S :, col : col + S] = block[: S // 2]
        joint[6 * S :, col + S : col + 2 * S] = block[S // 2 :]
    else:
        row, col = index // 4 * S, index % 4 * S
        joint[row : row + S, col : col + S] = block


def joint_block(joint, index):
    if joint.shape[0] == 6 * S + S // 2 and index >= 24:
        col = (index - 24) * 2 * S
        return jnp.concatenate([joint[6 * S :, col : col + S], joint[6 * S :, col + S : col + 2 * S]], axis=0)
    row, col = index // 4 * S, index % 4 * S
    return joint[row : row + S, col : col + S]


def joint_send(joint, row, t, block):
    if 4 <= t < 8:
        joint_put(joint, 4 * (3 - row) + 7 - t, block)
    if t >= 8 and (3 - row, 11 - t) in TRI:
        joint_put(joint, 16 + TRI.index((3 - row, 11 - t)), block)


def fill_table(cols, mask, table):
    for i in range(48):
        table[i] = -1
    for a in range(4):
        for s in range(8):
            active, row, t = place(cols, mask, a, s)
            table[jnp.where(active, 12 * row + t, 48)] = s


def source_row(row):
    return jnp.where(lax.axis_index("rep") == 1, 3 - row, row)


def slot_block(ref, table, row, t):
    slot = table[12 * row + t]
    block = ref[source_row(row), jnp.maximum(slot, 0)]
    return jnp.where(slot >= 0, block, jnp.zeros_like(block))


def x_slot_block(ref, table, diag, row, t):
    block = slot_block(ref, table, row, t)
    return (block.astype(F32) + diag).astype(BF) if t - 4 == row else block


def pack_kernel(cols_hbm, mask_hbm, h_hbm, x_hbm, joint_ref, xb_ref, table_ref, cols, mask, h_ref, x_ref, sems):
    pattern = [
        pltpu.make_async_copy(cols_hbm, cols, sems.at[0]),
        pltpu.make_async_copy(mask_hbm, mask, sems.at[1]),
    ]
    h_copy = pltpu.make_async_copy(h_hbm, h_ref, sems.at[2])
    x_copy = pltpu.make_async_copy(x_hbm, x_ref, sems.at[3])
    for copy in pattern + [h_copy, x_copy]:
        copy.start()
    for copy in pattern:
        copy.wait()
    fill_table(cols, mask, table_ref)
    diag = eye()

    h_copy.wait()
    for row in range(4):
        for t in range(4, 12):
            joint_send(joint_ref, row, t, slot_block(h_ref, table_ref, row, t))
    x_copy.wait()
    for index, (p, m) in enumerate(TRI):
        joint_put(joint_ref, 26 + index, slot_block(x_ref, table_ref, 3 - p, 11 - m))
    for row in range(4):
        for m in range(4):
            put(xb_ref, 3 - row, 3 - m, x_slot_block(x_ref, table_ref, diag, row, 4 + m))


def own_kernel(table, h_ref, x_ref, ho_ref, xo_ref):
    diag = eye()
    for row in range(4):
        for t in range(12):
            put(ho_ref, row, t, slot_block(h_ref, table, row, t))
            put(xo_ref, row, t, x_slot_block(x_ref, table, diag, row, t))


def spread_mine(get, square_ref):
    square_ref[H:, :H] = jnp.zeros((H, H), BF)
    square_ref[S : 2 * S, :S] = jnp.zeros((S, S), BF)
    square_ref[3 * S :, H : 3 * S] = jnp.zeros((S, S), BF)
    for index, (p, m) in enumerate(TRI):
        square_ref[p * S : (p + 1) * S, m * S : (m + 1) * S] = get(index)


def spread_twin(get, square_ref):
    square_ref[H:, H:] = jnp.zeros((H, H), BF)
    square_ref[S : 2 * S, 3 * S :] = jnp.zeros((S, S), BF)
    square_ref[3 * S :, S:H] = jnp.zeros((S, S), BF)
    for index, (p, m) in enumerate(TRI):
        square_ref[p * S : (p + 1) * S, (3 - m) * S : (4 - m) * S] = get(index)


def tile(ref, i, j):
    return ref[i * H : (i + 1) * H, j * H : (j + 1) * H]


def right_operand(ll, lc, own, rc, rr):
    def get(t, u):
        if t in OWN:
            if (t, u) in ((3, 1), (2, 5)):
                return None
            return own(t - 2, u)
        if t in LEFT:
            if u in LEFT:
                return tile(ll, t, u)
            if u in OWN and (t, u) != (1, 3):
                return tile(lc, t, u - 2)
            return None
        if u in RIGHT:
            return tile(rr, t - 4, u - 4)
        if u in OWN and (t, u) != (5, 2):
            return tile(rc, t - 4, u - 2)
        return None

    return get


def left_tile(ref, r, t):
    if (r, t) in ((1, 1), (0, 5)):
        return None
    return tile(ref, r, t)


def product(left, right, columns, finish):
    for u in columns:
        for r in range(2):
            if (r, u) in ((1, 1), (0, 5)):
                continue
            total = None
            for t in range(6):
                x = left(r, t)
                y = None if x is None else right(t, u)
                if y is None:
                    continue
                term = jnp.dot(x, y, preferred_element_type=F32)
                total = term if total is None else total + term
            finish(r, u, total)


def each_block(table_ref, r, u, total, store):
    for i in range(2):
        for j in range(2):
            row, t = 2 * r + i, 2 * u + j
            block = total[i * S : (i + 1) * S, j * S : (j + 1) * S]
            block = jnp.where(table_ref[12 * row + t] >= 0, block, 0.0)
            store(row, t, block)


def put(ref, row, t, block):
    ref[row * S : (row + 1) * S, t * S : (t + 1) * S] = block


def put_tile(ref, i, j, value):
    ref[i * H : (i + 1) * H, j * H : (j + 1) * H] = value


def mine_kernel(xo, ho, joint, part, rc):
    spread_mine(lambda i: joint_block(joint, 16 + i), rc)
    right = right_operand(None, None, lambda r, u: tile(ho, r, u), rc, joint)
    left = lambda r, t: None if t in LEFT else left_tile(xo, r, t)
    product(left, right, range(6), lambda r, u, total: put_tile(part, r, u, total))


def half_kernel(table, xo, twin, part, half_ref, lc):
    spread_twin(lambda i: joint_block(twin, 16 + i), lc)
    half_ref[H:, H:Q] = jnp.zeros((H, H), BF)
    half_ref[:H, 2 * Q + H :] = jnp.zeros((H, H), BF)
    right = right_operand(twin, lc, None, None, None)

    def keep(r, u, total):
        total = tile(part, r, u) if total is None else total + tile(part, r, u)
        each_block(table, r, u, total, lambda row, t, b: put(half_ref, row, t, b.astype(BF)))

    product(lambda r, t: left_tile(xo, r, t) if t in LEFT else None, right, range(6), keep)


def start_kernel(factor, table, half, xo, joint, twin, xb, band, send, side, xlc, xrc):
    spread_twin(lambda i: joint_block(twin, 26 + i), xlc)
    spread_mine(lambda i: joint_block(joint, 26 + i), xrc)
    right = right_operand(None, xlc, lambda r, u: tile(xo, r, u), xrc, xb)
    diag = eye()

    def start(r, u, total):
        def store(row, t, block):
            value = -factor * block
            if t - 4 == row:
                value = value + 0.5 * diag
            value = value.astype(BF)
            put(band, row, t, value)
            joint_send(send, row, t, value)
            if u in RIGHT and (3 - row, 11 - t) in TRI:
                side[TRI.index((3 - row, 11 - t))] = value

        each_block(table, r, u, total, store)

    product(lambda r, t: left_tile(half, r, t), right, OWN + RIGHT, start)


def mine_squares_kernel(table, band, joint, sq_r, part_l, sums, more, rc):
    spread_mine(lambda i: joint_block(joint, 16 + i), rc)
    sq_r[:H, H:] = jnp.zeros((H, H), BF)
    right = right_operand(None, None, lambda r, u: tile(band, r, u), rc, joint)

    def keep(r, u, total):
        if u in LEFT:
            put_tile(part_l, r, u, total)
        elif u in OWN:
            put_tile(sums, r, u - 2, total)
        else:
            each_block(table, r, u, total, lambda row, t, b: put(sq_r, row, t - 8, b.astype(BF)))

    product(lambda r, t: None if t in LEFT else left_tile(band, r, t), right, RIGHT + OWN + LEFT, keep)

    def square(r, t):
        return None if t not in RIGHT or (r, t) == (0, 5) else tile(sq_r, r, t - 4)

    product(square, right, OWN + RIGHT, lambda r, u, total: put_tile(more, r, u - 2, total))


def late_kernel(table, band, sq_r, part_l, sums, more, twin, lc, sq, finish, after=None):
    spread_twin(lambda i: joint_block(twin, 16 + i), lc)
    right = right_operand(twin, lc, lambda r, u: tile(band, r, u), None, None)

    for half in range(2):

        def only(left, *places):
            return lambda r, t: left(r, t) if r == half and t in places else None

        def keep(r, u, total):
            if r != half:
                return
            total = total + (tile(sums, r, u - 2) if u in OWN else tile(part_l, r, u))
            each_block(table, r, u, total, lambda row, t, b: put(sq, row, t, b.astype(BF)))

        def step(r, u, total):
            if r != half:
                return
            if u not in LEFT:
                total = total + tile(more, r, u - 2)

            def store(row, t, block):
                if u in RIGHT:
                    now = sq_r[row * S : (row + 1) * S, (t - 8) * S : (t - 7) * S]
                else:
                    now = sq[row * S : (row + 1) * S, t * S : (t + 1) * S]
                finish(row, t, (3.0 * now.astype(F32) - 2.0 * block).astype(BF))

            each_block(table, r, u, total, store)

        product(only(lambda r, t: left_tile(band, r, t), *LEFT), right, LEFT + OWN, keep)
        product(only(lambda r, t: left_tile(sq, r, t), *LEFT, *OWN), right, OWN + RIGHT + LEFT, step)
        if after:
            after(half)


def step_kernel(table, band, sq_r, part_l, sums, more, twin, new, send, lc, sq):
    new[H:, H:Q] = jnp.zeros((H, H), BF)
    new[:H, 2 * Q + H :] = jnp.zeros((H, H), BF)

    def finish(row, t, value):
        put(new, row, t, value)
        joint_send(send, row, t, value)

    late_kernel(table, band, sq_r, part_l, sums, more, twin, lc, sq, finish)


def last_kernel(cols, mask, table, band, sq_r, part_l, sums, more, twin, out_hbm, lc, sq, res, out, sems):
    core = lax.axis_index("rep")

    def copy(row):
        return pltpu.make_async_copy(out.at[row], out_hbm.at[source_row(row)], sems.at[row])

    def after(half):
        for row in (2 * half, 2 * half + 1):
            for s in range(4):
                active, unused, t = place(cols, mask, source_row(row), core * 4 + s)
                block = res[row * S : (row + 1) * S, at(t)]
                out[row, s] = jnp.where(active, block, jnp.zeros_like(block))
            copy(row).start()

    late_kernel(
        table, band, sq_r, part_l, sums, more, twin, lc, sq, lambda row, t, value: put(res, row, t, value), after
    )
    for row in range(4):
        copy(row).wait()


def join_kernel(band, side, out):
    out[:, Q:] = band[:, Q:]
    out[:H, 2 * Q + H :] = jnp.zeros((H, H), BF)
    spread_twin(lambda i: side[i], out.at[:, :Q])


def on_device(hamiltonian, x_correction, cols, mask):
    n = lax.axis_size("rows")
    factor = 0.6 / math.sqrt(cols.shape[1] * hamiltonian.shape[-1])
    outward = [(2 * i, 2 * i + 3) for i in range(n - 1)] + [(2 * i + 1, 2 * i - 2) for i in range(1, n)]

    def link(x):
        return lax.ppermute(x, ("rows", "rep"), outward)

    def swap(x):
        return lax.ppermute(x, "rep", [(0, 1), (1, 0)])

    square = pltpu.VMEM((Q, Q), BF)
    flops = 1 << 29
    hbm = pl.BlockSpec(memory_space=pltpu.HBM)

    index_table = jax.ShapeDtypeStruct((49,), jnp.int32)
    joint, xb, table = call(
        pack_kernel,
        [jax.ShapeDtypeStruct((9 * S, Q), BF), SQUARE, index_table],
        [VMEM, VMEM, SMEM],
        [hbm] * 4,
        [
            pltpu.SMEM(cols.shape, jnp.int32),
            pltpu.SMEM(mask.shape, jnp.int32),
            pltpu.VMEM(hamiltonian.shape, BF),
            pltpu.VMEM(x_correction.shape, BF),
            pltpu.SemaphoreType.DMA((4,)),
        ],
        flops,
        cols, mask, hamiltonian, x_correction,
        room=56,
    )
    joint_in = link(joint)
    xb_in = link(xb)
    ho, xo = call(
        own_kernel, [BANDED, BANDED], [VMEM] * 2, [SMEM, VMEM, VMEM], [], 0, table, hamiltonian, x_correction
    )
    twin = swap(joint_in)
    part = call(mine_kernel, WIDE, VMEM, [VMEM] * 3, [square], 64 * flops, xo, ho, joint_in)
    half = call(half_kernel, BANDED, VMEM, [SMEM] + [VMEM] * 3, [square], flops, table, xo, twin, part)
    band, send, side = call(
        lambda *refs: start_kernel(factor, *refs),
        [BANDED, SEND, CORNER],
        [VMEM] * 3,
        [SMEM] + [VMEM] * 5,
        [square] * 2,
        flops,
        table, half, xo, joint_in, twin, xb_in,
    )
    halo = link(send)
    band = call(join_kernel, BANDED, VMEM, [VMEM] * 2, [], 0, band, swap(side))
    for step in range(STEPS):
        if step > 0:
            halo = link(send)
        twin = swap(halo)
        sq_r, part_l, sums, more = call(
            mine_squares_kernel,
            [SQUARE, SUMS, SUMS, jax.ShapeDtypeStruct((Q, 2 * Q), F32)],
            [VMEM] * 4,
            [SMEM] + [VMEM] * 2,
            [square],
            64 * flops,
            table, band, halo,
        )
        operands = (table, band, sq_r, part_l, sums, more, twin)
        if step + 1 == STEPS:
            return call(
                last_kernel,
                jax.ShapeDtypeStruct((4, 4, S, S), BF),
                hbm,
                [SMEM] * 3 + [VMEM] * 6,
                [square, pltpu.VMEM((Q, 2 * Q), BF)]
                + [pltpu.VMEM((Q, 3 * Q), BF), pltpu.VMEM((4, 4, S, S), BF), pltpu.SemaphoreType.DMA((4,))],
                flops,
                cols, mask, *operands,
            )
        band, send = call(
            step_kernel,
            [BANDED, SEND],
            [VMEM] * 2,
            [SMEM] + [VMEM] * 6,
            [square, pltpu.VMEM((Q, 2 * Q), BF)],
            flops,
            *operands,
        )


def solution(mesh):
    return jax.shard_map(
        on_device,
        mesh=mesh,
        in_specs=(
            P("rows", None, None, None),
            P("rows", None, None, None),
            P("rows", None),
            P("rows", None),
        ),
        out_specs=P("rows", "rep", None, None),
        check_vma=False,
    )
```

```python
import math

import jax
import jax.numpy as jnp
from jax import lax
from jax.experimental import pallas as pl
from jax.experimental.pallas import tpu as pltpu
from jax.sharding import PartitionSpec as P

BAND = 4
STEPS = 2
S = 128
Q = 4 * S
H = 2 * S
TRI = [(p, m) for p in range(4) for m in range(p, 4)]
BF = jnp.bfloat16
F32 = jnp.float32
LEFT, OWN, RIGHT = (0, 1), (2, 3), (4, 5)

VMEM = pl.BlockSpec(memory_space=pltpu.VMEM)
SMEM = pl.BlockSpec(memory_space=pltpu.SMEM)
SQUARE = jax.ShapeDtypeStruct((Q, Q), BF)
CORNER = jax.ShapeDtypeStruct((len(TRI), S, S), BF)
BANDED = jax.ShapeDtypeStruct((Q, 3 * Q), BF)
SEND = jax.ShapeDtypeStruct((6 * S + S // 2, Q), BF)
SUMS = jax.ShapeDtypeStruct((Q, Q), F32)
WIDE = jax.ShapeDtypeStruct((Q, 3 * Q), F32)


def call(kernel, outs, out_specs, in_specs, scratch, flops, *args, room=24, alias=None):
    return pl.pallas_call(
        kernel,
        out_shape=outs,
        in_specs=in_specs,
        out_specs=out_specs,
        scratch_shapes=scratch,
        input_output_aliases=alias or {},
        compiler_params=pltpu.CompilerParams(vmem_limit_bytes=room << 20),
        cost_estimate=pl.CostEstimate(flops=flops, bytes_accessed=4 << 20, transcendentals=0),
    )(*args)


def place(cols_ref, mask_ref, a, s):
    first = lax.axis_index("rows") * 4 - BAND
    core = lax.axis_index("rep")
    k = cols_ref[a, s] - first
    k = jnp.clip(k, 0, 11)
    k = jnp.where(core == 1, 11 - k, k)
    row = jnp.where(core == 1, 3 - a, a)
    t = jnp.where(k < 4, 3 - k, k)
    return mask_ref[a, s] == 1, row, t


def at(index):
    return pl.ds(pl.multiple_of(index * S, S), S)


def eye():
    rows = lax.broadcasted_iota(jnp.int32, (S, S), 0)
    cols = lax.broadcasted_iota(jnp.int32, (S, S), 1)
    return (rows == cols).astype(F32)


def joint_put(joint, index, block):
    if index >= 24:
        col = (index - 24) * 2 * S
        joint[6 * S :, col : col + S] = block[: S // 2]
        joint[6 * S :, col + S : col + 2 * S] = block[S // 2 :]
    else:
        row, col = index // 4 * S, index % 4 * S
        joint[row : row + S, col : col + S] = block


def joint_block(joint, index):
    if index >= 24:
        col = (index - 24) * 2 * S
        return jnp.concatenate([joint[6 * S :, col : col + S], joint[6 * S :, col + S : col + 2 * S]], axis=0)
    row, col = index // 4 * S, index % 4 * S
    return joint[row : row + S, col : col + S]


def joint_send(joint, row, t, block):
    if 4 <= t < 8:
        joint_put(joint, 4 * (3 - row) + 7 - t, block)
    if t >= 8 and (3 - row, 11 - t) in TRI:
        joint_put(joint, 16 + TRI.index((3 - row, 11 - t)), block)


def fill_table(cols, mask, table):
    for i in range(48):
        table[i] = -1
    for a in range(4):
        for s in range(8):
            active, row, t = place(cols, mask, a, s)
            table[jnp.where(active, 12 * row + t, 48)] = s


def source_row(row):
    return jnp.where(lax.axis_index("rep") == 1, 3 - row, row)


def slot_block(ref, table, row, t):
    slot = table[12 * row + t]
    block = ref[source_row(row), jnp.maximum(slot, 0)]
    return jnp.where(slot >= 0, block, jnp.zeros_like(block))


def x_slot_block(ref, table, diag, row, t):
    block = slot_block(ref, table, row, t)
    return (block.astype(F32) + diag).astype(BF) if t - 4 == row else block


def pack_h_kernel(cols_hbm, mask_hbm, h_hbm, send, table, cols, mask, h_ref, sems):
    pattern = [
        pltpu.make_async_copy(cols_hbm, cols, sems.at[0]),
        pltpu.make_async_copy(mask_hbm, mask, sems.at[1]),
    ]
    rows = [pltpu.make_async_copy(h_hbm.at[source_row(row)], h_ref.at[row], sems.at[2 + row]) for row in range(4)]
    for copy in pattern + rows:
        copy.start()
    for copy in pattern:
        copy.wait()
    fill_table(cols, mask, table)
    for row in range(4):
        rows[row].wait()
        for t in range(4, 12):
            slot = table[12 * row + t]
            block = h_ref[row, jnp.maximum(slot, 0)]
            joint_send(send, row, t, jnp.where(slot >= 0, block, jnp.zeros_like(block)))


def pack_x_kernel(table, x_ref, xa, xb):
    diag = eye()
    for index, (p, m) in enumerate(TRI):
        xa[index] = slot_block(x_ref, table, 3 - p, 11 - m)
    for row in range(4):
        for m in range(4):
            put(xb, 3 - row, 3 - m, x_slot_block(x_ref, table, diag, row, 4 + m))


def own_kernel(table, h_ref, x_ref, ho_ref, xo_ref, marks):
    diag = eye()
    for i in range(48):
        marks[i : i + 1, :] = jnp.full((1, S), jnp.where(table[i] >= 0, 1.0, 0.0), F32)
    for row in range(4):
        for t in range(12):
            put(ho_ref, row, t, slot_block(h_ref, table, row, t))
            put(xo_ref, row, t, x_slot_block(x_ref, table, diag, row, t))


def spread_mine(get, square_ref):
    square_ref[H:, :H] = jnp.zeros((H, H), BF)
    square_ref[S : 2 * S, :S] = jnp.zeros((S, S), BF)
    square_ref[3 * S :, H : 3 * S] = jnp.zeros((S, S), BF)
    for index, (p, m) in enumerate(TRI):
        square_ref[p * S : (p + 1) * S, m * S : (m + 1) * S] = get(index)


def spread_twin(get, square_ref):
    square_ref[H:, H:] = jnp.zeros((H, H), BF)
    square_ref[S : 2 * S, 3 * S :] = jnp.zeros((S, S), BF)
    square_ref[3 * S :, S:H] = jnp.zeros((S, S), BF)
    for index, (p, m) in enumerate(TRI):
        square_ref[p * S : (p + 1) * S, (3 - m) * S : (4 - m) * S] = get(index)


def tile(ref, i, j):
    return ref[i * H : (i + 1) * H, j * H : (j + 1) * H]


def right_operand(ll, lc, own, rc, rr):
    def get(t, u):
        if t in OWN:
            if (t, u) in ((3, 1), (2, 5)):
                return None
            return own(t - 2, u)
        if t in LEFT:
            if u in LEFT:
                return tile(ll, t, u)
            if u in OWN and (t, u) != (1, 3):
                return tile(lc, t, u - 2)
            return None
        if u in RIGHT:
            return tile(rr, t - 4, u - 4)
        if u in OWN and (t, u) != (5, 2):
            return tile(rc, t - 4, u - 2)
        return None

    return get


def left_tile(ref, r, t):
    if (r, t) in ((1, 1), (0, 5)):
        return None
    return tile(ref, r, t)


def product(left, right, columns, finish):
    for u in columns:
        for r in range(2):
            if (r, u) in ((1, 1), (0, 5)):
                continue
            xs, ys = [], []
            for t in range(6):
                x = left(r, t)
                y = None if x is None else right(t, u)
                if y is not None:
                    xs.append(x)
                    ys.append(y)
            total = None
            if xs:
                x, y = jnp.concatenate(xs, axis=1), jnp.concatenate(ys, axis=0)
                total = jnp.dot(x, y, preferred_element_type=F32)
            finish(r, u, total)


def each_block(table_ref, r, u, total, store):
    for i in range(2):
        for j in range(2):
            row, t = 2 * r + i, 2 * u + j
            block = total[i * S : (i + 1) * S, j * S : (j + 1) * S]
            block = jnp.where(table_ref[12 * row + t : 12 * row + t + 1, :] > 0.0, block, 0.0)
            store(row, t, block)


def put(ref, row, t, block):
    ref[row * S : (row + 1) * S, t * S : (t + 1) * S] = block


def put_tile(ref, i, j, value):
    ref[i * H : (i + 1) * H, j * H : (j + 1) * H] = value


def mine_kernel(xo, ho, joint, part, rc):
    spread_mine(lambda i: joint_block(joint, 16 + i), rc)
    right = right_operand(None, None, lambda r, u: tile(ho, r, u), rc, joint)
    left = lambda r, t: None if t in LEFT else left_tile(xo, r, t)
    product(left, right, range(6), lambda r, u, total: put_tile(part, r, u, total))


def spread_kernel(xa, part, copy, square):
    copy[...] = xa[...]
    spread_mine(lambda i: xa[i], square)


def half_kernel(table, xo, twin, part, half_ref, lc):
    spread_twin(lambda i: joint_block(twin, 16 + i), lc)
    half_ref[H:, H:Q] = jnp.zeros((H, H), BF)
    half_ref[:H, 2 * Q + H :] = jnp.zeros((H, H), BF)
    right = right_operand(twin, lc, None, None, None)

    def keep(r, u, total):
        total = tile(part, r, u) if total is None else total + tile(part, r, u)
        each_block(table, r, u, total, lambda row, t, b: put(half_ref, row, t, b.astype(BF)))

    product(lambda r, t: left_tile(xo, r, t) if t in LEFT else None, right, range(6), keep)


def center_kernel(factor, table, half, xo, xrc, xa2, band, send, xlc):
    spread_twin(lambda i: xa2[i], xlc)
    right = right_operand(None, xlc, lambda r, u: tile(xo, r, u), xrc, None)
    diag = eye()

    def start(r, u, total):
        def store(row, t, block):
            value = -factor * block
            if t - 4 == row:
                value = value + 0.5 * diag
            value = value.astype(BF)
            put(band, row, t, value)
            joint_send(send, row, t, value)

        each_block(table, r, u, total, store)

    product(lambda r, t: left_tile(half, r, t), right, OWN, start)


def side_kernel(factor, table, half, xo, xb, band_in, send_in, band, send, side):
    right = right_operand(None, None, lambda r, u: tile(xo, r, u), None, xb)

    def start(r, u, total):
        def store(row, t, block):
            value = (-factor * block).astype(BF)
            put(band, row, t, value)
            joint_send(send, row, t, value)
            if (3 - row, 11 - t) in TRI:
                side[TRI.index((3 - row, 11 - t))] = value

        each_block(table, r, u, total, store)

    product(lambda r, t: left_tile(half, r, t), right, RIGHT, start)


def mine_squares_kernel(table, band, joint, sq_r, part_l, sums, more, rc):
    spread_mine(lambda i: joint_block(joint, 16 + i), rc)
    sq_r[:H, H:] = jnp.zeros((H, H), BF)
    right = right_operand(None, None, lambda r, u: tile(band, r, u), rc, joint)

    def keep(r, u, total):
        if u in LEFT:
            put_tile(part_l, r, u, total)
        elif u in OWN:
            put_tile(sums, r, u - 2, total)
        else:
            each_block(table, r, u, total, lambda row, t, b: put(sq_r, row, t - 8, b.astype(BF)))

    product(lambda r, t: None if t in LEFT else left_tile(band, r, t), right, RIGHT + OWN + LEFT, keep)

    def square(r, t):
        return None if t not in RIGHT or (r, t) == (0, 5) else tile(sq_r, r, t - 4)

    product(square, right, OWN + RIGHT, lambda r, u, total: put_tile(more, r, u - 2, total))


def late_kernel(columns, table, band, sq_r, part_l, sums, more, twin, lc, sq, finish, after=None):
    spread_twin(lambda i: joint_block(twin, 16 + i), lc)
    right = right_operand(twin, lc, lambda r, u: tile(band, r, u), None, None)

    for half in range(2):

        def only(left, *places):
            return lambda r, t: left(r, t) if r == half and t in places else None

        def keep(r, u, total):
            if r != half:
                return
            total = total + (tile(sums, r, u - 2) if u in OWN else tile(part_l, r, u))
            each_block(table, r, u, total, lambda row, t, b: put(sq, row, t, b.astype(BF)))

        def step(r, u, total):
            if r != half:
                return
            if u not in LEFT:
                total = total + tile(more, r, u - 2)

            def store(row, t, block):
                if u in RIGHT:
                    now = sq_r[row * S : (row + 1) * S, (t - 8) * S : (t - 7) * S]
                else:
                    now = sq[row * S : (row + 1) * S, t * S : (t + 1) * S]
                finish(row, t, (3.0 * now.astype(F32) - 2.0 * block).astype(BF))

            each_block(table, r, u, total, store)

        product(only(lambda r, t: left_tile(band, r, t), *LEFT), right, LEFT + OWN, keep)
        product(only(lambda r, t: left_tile(sq, r, t), *LEFT, *OWN), right, columns, step)
        if after:
            after(half)


def step_kernel(table, band, sq_r, part_l, sums, more, twin, new, send, sq, lc):
    def finish(row, t, value):
        put(new, row, t, value)
        joint_send(send, row, t, value)

    late_kernel(OWN + RIGHT, table, band, sq_r, part_l, sums, more, twin, lc, sq, finish)


def step_left_kernel(table, band, sq, twin, new_in, new):
    new[H:, H:Q] = jnp.zeros((H, H), BF)
    new[:H, 2 * Q + H :] = jnp.zeros((H, H), BF)
    right = right_operand(twin, None, lambda r, u: tile(band, r, u), None, None)

    def step(r, u, total):
        def store(row, t, block):
            now = sq[row * S : (row + 1) * S, t * S : (t + 1) * S]
            put(new, row, t, (3.0 * now.astype(F32) - 2.0 * block).astype(BF))

        each_block(table, r, u, total, store)

    product(lambda r, t: None if t in RIGHT else left_tile(sq, r, t), right, LEFT, step)


def last_kernel(cols_hbm, mask_hbm, table, band, sq_r, part_l, sums, more, twin, out_hbm, *scratch):
    lc, sq, res, out, sems, cols, mask = scratch
    core = lax.axis_index("rep")
    pattern = [
        pltpu.make_async_copy(cols_hbm, cols, sems.at[4]),
        pltpu.make_async_copy(mask_hbm, mask, sems.at[5]),
    ]
    for one in pattern:
        one.start()

    def copy(row):
        return pltpu.make_async_copy(out.at[row], out_hbm.at[source_row(row)], sems.at[row])

    def after(half):
        if half == 0:
            for one in pattern:
                one.wait()
        for row in (2 * half, 2 * half + 1):
            for s in range(4):
                active, unused, t = place(cols, mask, source_row(row), core * 4 + s)
                block = res[row * S : (row + 1) * S, at(t)]
                out[row, s] = jnp.where(active, block, jnp.zeros_like(block))
            copy(row).start()

    late_kernel(
        LEFT + OWN + RIGHT, table, band, sq_r, part_l, sums, more, twin, lc, sq, lambda row, t, value: put(res, row, t, value), after
    )
    for row in range(4):
        copy(row).wait()


def join_kernel(band, side, out):
    out[:, Q:] = band[:, Q:]
    out[:H, 2 * Q + H :] = jnp.zeros((H, H), BF)
    spread_twin(lambda i: side[i], out.at[:, :Q])


def on_device(hamiltonian, x_correction, cols, mask):
    n = lax.axis_size("rows")
    factor = 0.6 / math.sqrt(cols.shape[1] * hamiltonian.shape[-1])
    outward = [(2 * i, 2 * i + 3) for i in range(n - 1)] + [(2 * i + 1, 2 * i - 2) for i in range(1, n)]

    def link(x):
        return lax.ppermute(x, ("rows", "rep"), outward)

    def swap(x):
        return lax.ppermute(x, "rep", [(0, 1), (1, 0)])

    square = pltpu.VMEM((Q, Q), BF)
    flops = 1 << 29
    hbm = pl.BlockSpec(memory_space=pltpu.HBM)

    index_table = jax.ShapeDtypeStruct((49,), jnp.int32)
    h_send, table = call(
        pack_h_kernel,
        [SEND, index_table],
        [VMEM, SMEM],
        [hbm] * 3,
        [
            pltpu.SMEM(cols.shape, jnp.int32),
            pltpu.SMEM(mask.shape, jnp.int32),
            pltpu.VMEM(hamiltonian.shape, BF),
            pltpu.SemaphoreType.DMA((6,)),
        ],
        flops,
        cols, mask, hamiltonian,
        room=56,
    )
    h_halo = link(h_send)
    xa, xb = call(pack_x_kernel, [CORNER, SQUARE], [VMEM] * 2, [SMEM, VMEM], [], 0, table, x_correction)
    xa_halo = link(xa)
    xb_halo = link(xb)
    ho, xo, marks = call(
        own_kernel,
        [BANDED, BANDED, jax.ShapeDtypeStruct((48, S), F32)],
        [VMEM] * 3,
        [SMEM, VMEM, VMEM],
        [],
        0,
        table, hamiltonian, x_correction,
    )
    h_twin = swap(h_halo)
    part = call(mine_kernel, WIDE, VMEM, [VMEM] * 3, [square], 64 * flops, xo, ho, h_halo)
    xa_copy, x_corner = call(spread_kernel, [CORNER, SQUARE], [VMEM] * 2, [VMEM] * 2, [], 0, xa_halo, part)
    xa_twin = swap(xa_copy)
    half = call(half_kernel, BANDED, VMEM, [VMEM] + [VMEM] * 3, [square], 16 * flops, marks, xo, h_twin, part)
    band, send = call(
        lambda *refs: center_kernel(factor, *refs),
        [BANDED, SEND],
        [VMEM] * 2,
        [VMEM] * 5,
        [square],
        flops,
        marks, half, xo, x_corner, xa_twin,
    )
    band, send, side = call(
        lambda *refs: side_kernel(factor, *refs),
        [BANDED, SEND, CORNER],
        [VMEM] * 3,
        [VMEM] * 6,
        [],
        flops,
        marks, half, xo, xb_halo, band, send,
        alias={4: 0, 5: 1},
    )
    halo = link(send)
    band = call(join_kernel, BANDED, VMEM, [VMEM] * 2, [], 0, band, swap(side))
    for step in range(STEPS):
        if step > 0:
            halo = link(send)
        twin = swap(halo)
        sq_r, part_l, sums, more = call(
            mine_squares_kernel,
            [SQUARE, SUMS, SUMS, jax.ShapeDtypeStruct((Q, 2 * Q), F32)],
            [VMEM] * 4,
            [VMEM] + [VMEM] * 2,
            [square],
            64 * flops,
            marks, band, halo,
        )
        operands = (marks, band, sq_r, part_l, sums, more, twin)
        if step + 1 == STEPS:
            return call(
                last_kernel,
                jax.ShapeDtypeStruct((4, 4, S, S), BF),
                hbm,
                [hbm] * 2 + [VMEM] * 7,
                [square, pltpu.VMEM((Q, 2 * Q), BF)]
                + [pltpu.VMEM((Q, 3 * Q), BF), pltpu.VMEM((4, 4, S, S), BF), pltpu.SemaphoreType.DMA((6,))]
                + [pltpu.SMEM(cols.shape, jnp.int32), pltpu.SMEM(mask.shape, jnp.int32)],
                flops,
                cols, mask, *operands,
            )
        new, send, sq = call(
            step_kernel,
            [BANDED, SEND, jax.ShapeDtypeStruct((Q, 2 * Q), BF)],
            [VMEM] * 3,
            [VMEM] * 7,
            [square],
            flops,
            *operands,
        )
        band = call(
            step_left_kernel, BANDED, VMEM, [VMEM] * 5, [], 0, marks, band, sq, twin, new, alias={4: 0}
        )


def solution(mesh):
    return jax.shard_map(
        on_device,
        mesh=mesh,
        in_specs=(
            P("rows", None, None, None),
            P("rows", None, None, None),
            P("rows", None),
            P("rows", None),
        ),
        out_specs=P("rows", "rep", None, None),
        check_vma=False,
    )
```

```python
import math

import jax
import jax.numpy as jnp
from jax import lax
from jax.experimental import pallas as pl
from jax.experimental.pallas import tpu as pltpu
from jax.sharding import PartitionSpec as P

BAND = 4
STEPS = 2
S = 128
Q = 4 * S
H = 2 * S
TRI = [(p, m) for p in range(4) for m in range(p, 4)]
BF = jnp.bfloat16
F32 = jnp.float32
LEFT, OWN, RIGHT = (0, 1), (2, 3), (4, 5)

VMEM = pl.BlockSpec(memory_space=pltpu.VMEM)
SMEM = pl.BlockSpec(memory_space=pltpu.SMEM)
SQUARE = jax.ShapeDtypeStruct((Q, Q), BF)
CORNER = jax.ShapeDtypeStruct((len(TRI), S, S), BF)
BANDED = jax.ShapeDtypeStruct((Q, 3 * Q), BF)
SEND = jax.ShapeDtypeStruct((6 * S + S // 2, Q), BF)
SUMS = jax.ShapeDtypeStruct((Q, Q), F32)
WIDE = jax.ShapeDtypeStruct((Q, 3 * Q), F32)


def call(kernel, outs, out_specs, in_specs, scratch, flops, *args, room=24, alias=None):
    return pl.pallas_call(
        kernel,
        out_shape=outs,
        in_specs=in_specs,
        out_specs=out_specs,
        scratch_shapes=scratch,
        input_output_aliases=alias or {},
        compiler_params=pltpu.CompilerParams(vmem_limit_bytes=room << 20),
        cost_estimate=pl.CostEstimate(flops=flops, bytes_accessed=4 << 20, transcendentals=0),
    )(*args)


def place(cols_ref, mask_ref, a, s):
    first = lax.axis_index("rows") * 4 - BAND
    core = lax.axis_index("rep")
    k = cols_ref[a, s] - first
    k = jnp.clip(k, 0, 11)
    k = jnp.where(core == 1, 11 - k, k)
    row = jnp.where(core == 1, 3 - a, a)
    t = jnp.where(k < 4, 3 - k, k)
    return mask_ref[a, s] == 1, row, t


def at(index):
    return pl.ds(pl.multiple_of(index * S, S), S)


def eye():
    rows = lax.broadcasted_iota(jnp.int32, (S, S), 0)
    cols = lax.broadcasted_iota(jnp.int32, (S, S), 1)
    return (rows == cols).astype(F32)


def joint_put(joint, index, block):
    if index >= 24:
        col = (index - 24) * 2 * S
        joint[6 * S :, col : col + S] = block[: S // 2]
        joint[6 * S :, col + S : col + 2 * S] = block[S // 2 :]
    else:
        row, col = index // 4 * S, index % 4 * S
        joint[row : row + S, col : col + S] = block


def joint_block(joint, index):
    if index >= 24:
        col = (index - 24) * 2 * S
        return jnp.concatenate([joint[6 * S :, col : col + S], joint[6 * S :, col + S : col + 2 * S]], axis=0)
    row, col = index // 4 * S, index % 4 * S
    return joint[row : row + S, col : col + S]


def joint_send(joint, row, t, block):
    if 4 <= t < 8:
        joint_put(joint, 4 * (3 - row) + 7 - t, block)
    if t >= 8 and (3 - row, 11 - t) in TRI:
        joint_put(joint, 16 + TRI.index((3 - row, 11 - t)), block)


def fill_table(cols, mask, table):
    for i in range(48):
        table[i] = -1
    for a in range(4):
        for s in range(8):
            active, row, t = place(cols, mask, a, s)
            table[jnp.where(active, 12 * row + t, 48)] = s


def source_row(row):
    return jnp.where(lax.axis_index("rep") == 1, 3 - row, row)


def row_block(ref, table, row, t, source=None):
    slot = table[12 * row + t]
    block = ref[row if source is None else source, jnp.maximum(slot, 0)]
    return jnp.where(slot >= 0, block, jnp.zeros_like(block))


def slot_block(ref, table, row, t):
    return row_block(ref, table, row, t, source_row(row))


def x_slot_block(ref, table, diag, row, t):
    block = slot_block(ref, table, row, t)
    return (block.astype(F32) + diag).astype(BF) if t - 4 == row else block


def pack_h_kernel(cols_hbm, mask_hbm, h_hbm, send, table, h_ref, cols, mask, sems):
    pattern = [
        pltpu.make_async_copy(cols_hbm, cols, sems.at[0]),
        pltpu.make_async_copy(mask_hbm, mask, sems.at[1]),
    ]
    rows = [pltpu.make_async_copy(h_hbm.at[source_row(row)], h_ref.at[row], sems.at[2 + row]) for row in range(4)]
    for copy in pattern + rows:
        copy.start()
    for copy in pattern:
        copy.wait()
    fill_table(cols, mask, table)
    for row in range(4):
        rows[row].wait()
        for t in range(4, 12):
            joint_send(send, row, t, row_block(h_ref, table, row, t))


def pack_x_kernel(table, x_ref, xa, xb, marks):
    diag = eye()
    for index, (p, m) in enumerate(TRI):
        xa[index] = slot_block(x_ref, table, 3 - p, 11 - m)
    for row in range(4):
        for m in range(4):
            put(xb, 3 - row, 3 - m, x_slot_block(x_ref, table, diag, row, 4 + m))
    for i in range(48):
        marks[i : i + 1, :] = jnp.full((1, S), jnp.where(table[i] >= 0, 1.0, 0.0), F32)


def spread_mine(get, square_ref):
    square_ref[H:, :H] = jnp.zeros((H, H), BF)
    square_ref[S : 2 * S, :S] = jnp.zeros((S, S), BF)
    square_ref[3 * S :, H : 3 * S] = jnp.zeros((S, S), BF)
    for index, (p, m) in enumerate(TRI):
        square_ref[p * S : (p + 1) * S, m * S : (m + 1) * S] = get(index)


def spread_twin(get, square_ref):
    square_ref[H:, H:] = jnp.zeros((H, H), BF)
    square_ref[S : 2 * S, 3 * S :] = jnp.zeros((S, S), BF)
    square_ref[3 * S :, S:H] = jnp.zeros((S, S), BF)
    for index, (p, m) in enumerate(TRI):
        square_ref[p * S : (p + 1) * S, (3 - m) * S : (4 - m) * S] = get(index)


def tile(ref, i, j):
    return ref[i * H : (i + 1) * H, j * H : (j + 1) * H]


def right_operand(ll, lc, own, rc, rr):
    def get(t, u):
        if t in OWN:
            if (t, u) in ((3, 1), (2, 5)):
                return None
            return own(t - 2, u)
        if t in LEFT:
            if u in LEFT:
                return tile(ll, t, u)
            if u in OWN and (t, u) != (1, 3):
                return tile(lc, t, u - 2)
            return None
        if u in RIGHT:
            return tile(rr, t - 4, u - 4)
        if u in OWN and (t, u) != (5, 2):
            return tile(rc, t - 4, u - 2)
        return None

    return get


def left_tile(ref, r, t):
    if (r, t) in ((1, 1), (0, 5)):
        return None
    return tile(ref, r, t)


def product(left, right, columns, finish):
    for u in columns:
        for r in range(2):
            if (r, u) in ((1, 1), (0, 5)):
                continue
            xs, ys = [], []
            for t in range(6):
                x = left(r, t)
                y = None if x is None else right(t, u)
                if y is not None:
                    xs.append(x)
                    ys.append(y)
            total = None
            if xs:
                x, y = jnp.concatenate(xs, axis=1), jnp.concatenate(ys, axis=0)
                total = jnp.dot(x, y, preferred_element_type=F32)
            finish(r, u, total)


def each_block(table_ref, r, u, total, store):
    for i in range(2):
        for j in range(2):
            row, t = 2 * r + i, 2 * u + j
            block = total[i * S : (i + 1) * S, j * S : (j + 1) * S]
            block = jnp.where(table_ref[12 * row + t : 12 * row + t + 1, :] > 0.0, block, 0.0)
            store(row, t, block)


def put(ref, row, t, block):
    ref[row * S : (row + 1) * S, t * S : (t + 1) * S] = block


def put_tile(ref, i, j, value):
    ref[i * H : (i + 1) * H, j * H : (j + 1) * H] = value


def mine_kernel(table, h_ref, x_ref, joint, xo, part, ho, rc):
    diag = eye()
    for row in range(4):
        for t in range(12):
            put(ho, row, t, row_block(h_ref, table, row, t))
            put(xo, row, t, x_slot_block(x_ref, table, diag, row, t))
    spread_mine(lambda i: joint_block(joint, 16 + i), rc)
    right = right_operand(None, None, lambda r, u: tile(ho, r, u), rc, joint)
    left = lambda r, t: None if t in LEFT else left_tile(xo, r, t)
    product(left, right, range(6), lambda r, u, total: put_tile(part, r, u, total))


def spread_kernel(xa, part, copy, square):
    copy[...] = xa[...]
    spread_mine(lambda i: xa[i], square)


def half_kernel(table, xo, twin, part, half_ref, lc):
    spread_twin(lambda i: joint_block(twin, 16 + i), lc)
    half_ref[H:, H:Q] = jnp.zeros((H, H), BF)
    half_ref[:H, 2 * Q + H :] = jnp.zeros((H, H), BF)
    right = right_operand(twin, lc, None, None, None)

    def keep(r, u, total):
        total = tile(part, r, u) if total is None else total + tile(part, r, u)
        each_block(table, r, u, total, lambda row, t, b: put(half_ref, row, t, b.astype(BF)))

    product(lambda r, t: left_tile(xo, r, t) if t in LEFT else None, right, range(6), keep)


def center_kernel(factor, table, half, xo, xrc, xa2, band, send, xlc):
    spread_twin(lambda i: xa2[i], xlc)
    right = right_operand(None, xlc, lambda r, u: tile(xo, r, u), xrc, None)
    diag = eye()

    def start(r, u, total):
        def store(row, t, block):
            value = -factor * block
            if t - 4 == row:
                value = value + 0.5 * diag
            value = value.astype(BF)
            put(band, row, t, value)
            joint_send(send, row, t, value)

        each_block(table, r, u, total, store)

    product(lambda r, t: left_tile(half, r, t), right, OWN, start)


def side_kernel(factor, table, half, xo, xb, band_in, send_in, band, send, side):
    right = right_operand(None, None, lambda r, u: tile(xo, r, u), None, xb)

    def start(r, u, total):
        def store(row, t, block):
            value = (-factor * block).astype(BF)
            put(band, row, t, value)
            joint_send(send, row, t, value)
            if (3 - row, 11 - t) in TRI:
                side[TRI.index((3 - row, 11 - t))] = value

        each_block(table, r, u, total, store)

    product(lambda r, t: left_tile(half, r, t), right, RIGHT, start)


def mine_squares_kernel(table, band, joint, sq_r, part_l, sums, more, rc):
    spread_mine(lambda i: joint_block(joint, 16 + i), rc)
    sq_r[:H, H:] = jnp.zeros((H, H), BF)
    right = right_operand(None, None, lambda r, u: tile(band, r, u), rc, joint)

    def keep(r, u, total):
        if u in LEFT:
            put_tile(part_l, r, u, total)
        elif u in OWN:
            put_tile(sums, r, u - 2, total)
        else:
            each_block(table, r, u, total, lambda row, t, b: put(sq_r, row, t - 8, b.astype(BF)))

    product(lambda r, t: None if t in LEFT else left_tile(band, r, t), right, RIGHT + OWN + LEFT, keep)

    def square(r, t):
        return None if t not in RIGHT or (r, t) == (0, 5) else tile(sq_r, r, t - 4)

    product(square, right, OWN + RIGHT, lambda r, u, total: put_tile(more, r, u - 2, total))


def late_kernel(columns, table, band, sq_r, part_l, sums, more, twin, lc, sq, finish, after=None):
    spread_twin(lambda i: joint_block(twin, 16 + i), lc)
    right = right_operand(twin, lc, lambda r, u: tile(band, r, u), None, None)

    for half in range(2):

        def only(left, *places):
            return lambda r, t: left(r, t) if r == half and t in places else None

        def keep(r, u, total):
            if r != half:
                return
            total = total + (tile(sums, r, u - 2) if u in OWN else tile(part_l, r, u))
            each_block(table, r, u, total, lambda row, t, b: put(sq, row, t, b.astype(BF)))

        def step(r, u, total):
            if r != half:
                return
            if u not in LEFT:
                total = total + tile(more, r, u - 2)

            def store(row, t, block):
                if u in RIGHT:
                    now = sq_r[row * S : (row + 1) * S, (t - 8) * S : (t - 7) * S]
                else:
                    now = sq[row * S : (row + 1) * S, t * S : (t + 1) * S]
                finish(row, t, (3.0 * now.astype(F32) - 2.0 * block).astype(BF))

            each_block(table, r, u, total, store)

        product(only(lambda r, t: left_tile(band, r, t), *LEFT), right, LEFT + OWN, keep)
        product(only(lambda r, t: left_tile(sq, r, t), *LEFT, *OWN), right, columns, step)
        if after:
            after(half)


def step_kernel(table, band, sq_r, part_l, sums, more, twin, new, send, sq, lc):
    def finish(row, t, value):
        put(new, row, t, value)
        joint_send(send, row, t, value)

    late_kernel(OWN + RIGHT, table, band, sq_r, part_l, sums, more, twin, lc, sq, finish)


def step_left_kernel(table, band, sq, twin, new_in, new):
    new[H:, H:Q] = jnp.zeros((H, H), BF)
    new[:H, 2 * Q + H :] = jnp.zeros((H, H), BF)
    right = right_operand(twin, None, lambda r, u: tile(band, r, u), None, None)

    def step(r, u, total):
        def store(row, t, block):
            now = sq[row * S : (row + 1) * S, t * S : (t + 1) * S]
            put(new, row, t, (3.0 * now.astype(F32) - 2.0 * block).astype(BF))

        each_block(table, r, u, total, store)

    product(lambda r, t: None if t in RIGHT else left_tile(sq, r, t), right, LEFT, step)


def last_kernel(cols_hbm, mask_hbm, table, band, sq_r, part_l, sums, more, twin, out_hbm, *scratch):
    lc, sq, res, out, sems, cols, mask = scratch
    core = lax.axis_index("rep")
    pattern = [
        pltpu.make_async_copy(cols_hbm, cols, sems.at[4]),
        pltpu.make_async_copy(mask_hbm, mask, sems.at[5]),
    ]
    for one in pattern:
        one.start()

    def copy(row):
        return pltpu.make_async_copy(out.at[row], out_hbm.at[source_row(row)], sems.at[row])

    def after(half):
        if half == 0:
            for one in pattern:
                one.wait()
        for row in (2 * half, 2 * half + 1):
            for s in range(4):
                active, unused, t = place(cols, mask, source_row(row), core * 4 + s)
                block = res[row * S : (row + 1) * S, at(t)]
                out[row, s] = jnp.where(active, block, jnp.zeros_like(block))
            copy(row).start()

    late_kernel(
        LEFT + OWN + RIGHT, table, band, sq_r, part_l, sums, more, twin, lc, sq, lambda row, t, value: put(res, row, t, value), after
    )
    for row in range(4):
        copy(row).wait()


def join_kernel(band, side, out):
    out[:, Q:] = band[:, Q:]
    out[:H, 2 * Q + H :] = jnp.zeros((H, H), BF)
    spread_twin(lambda i: side[i], out.at[:, :Q])


def on_device(hamiltonian, x_correction, cols, mask):
    n = lax.axis_size("rows")
    factor = 0.6 / math.sqrt(cols.shape[1] * hamiltonian.shape[-1])
    outward = [(2 * i, 2 * i + 3) for i in range(n - 1)] + [(2 * i + 1, 2 * i - 2) for i in range(1, n)]

    def link(x):
        return lax.ppermute(x, ("rows", "rep"), outward)

    def swap(x):
        return lax.ppermute(x, "rep", [(0, 1), (1, 0)])

    square = pltpu.VMEM((Q, Q), BF)
    flops = 1 << 29
    hbm = pl.BlockSpec(memory_space=pltpu.HBM)

    index_table = jax.ShapeDtypeStruct((49,), jnp.int32)
    h_send, table, h_rows = call(
        pack_h_kernel,
        [SEND, index_table, jax.ShapeDtypeStruct(hamiltonian.shape, BF)],
        [VMEM, SMEM, VMEM],
        [hbm] * 3,
        [
            pltpu.SMEM(cols.shape, jnp.int32),
            pltpu.SMEM(mask.shape, jnp.int32),
            pltpu.SemaphoreType.DMA((6,)),
        ],
        flops,
        *(pltpu.with_memory_space_constraint(x, pltpu.HBM) for x in (cols, mask, hamiltonian)),
    )
    h_halo = link(h_send)
    xa, xb, marks = call(
        pack_x_kernel,
        [CORNER, SQUARE, jax.ShapeDtypeStruct((48, S), F32)],
        [VMEM] * 3,
        [SMEM, VMEM],
        [],
        0,
        table, x_correction,
    )
    xa_halo = link(xa)
    xb_halo = link(xb)
    h_twin = swap(h_halo)
    xo, part = call(
        mine_kernel,
        [BANDED, WIDE],
        [VMEM] * 2,
        [SMEM] + [VMEM] * 3,
        [pltpu.VMEM((Q, 3 * Q), BF), square],
        64 * flops,
        table, h_rows, x_correction, h_halo,
    )
    xa_copy, x_corner = call(spread_kernel, [CORNER, SQUARE], [VMEM] * 2, [VMEM] * 2, [], 0, xa_halo, part)
    xa_twin = swap(xa_copy)
    half = call(half_kernel, BANDED, VMEM, [VMEM] + [VMEM] * 3, [square], 16 * flops, marks, xo, h_twin, part)
    band, send = call(
        lambda *refs: center_kernel(factor, *refs),
        [BANDED, SEND],
        [VMEM] * 2,
        [VMEM] * 5,
        [square],
        flops,
        marks, half, xo, x_corner, xa_twin,
    )
    band, send, side = call(
        lambda *refs: side_kernel(factor, *refs),
        [BANDED, SEND, CORNER],
        [VMEM] * 3,
        [VMEM] * 6,
        [],
        flops,
        marks, half, xo, xb_halo, band, send,
        alias={4: 0, 5: 1},
    )
    halo = link(send)
    band = call(join_kernel, BANDED, VMEM, [VMEM] * 2, [], 0, band, swap(side))
    for step in range(STEPS):
        if step > 0:
            halo = link(send)
        twin = swap(halo)
        sq_r, part_l, sums, more = call(
            mine_squares_kernel,
            [SQUARE, SUMS, SUMS, jax.ShapeDtypeStruct((Q, 2 * Q), F32)],
            [VMEM] * 4,
            [VMEM] + [VMEM] * 2,
            [square],
            64 * flops,
            marks, band, halo,
        )
        operands = (marks, band, sq_r, part_l, sums, more, twin)
        if step + 1 == STEPS:
            return call(
                last_kernel,
                jax.ShapeDtypeStruct((4, 4, S, S), BF),
                hbm,
                [hbm] * 2 + [VMEM] * 7,
                [square, pltpu.VMEM((Q, 2 * Q), BF)]
                + [pltpu.VMEM((Q, 3 * Q), BF), pltpu.VMEM((4, 4, S, S), BF), pltpu.SemaphoreType.DMA((6,))]
                + [pltpu.SMEM(cols.shape, jnp.int32), pltpu.SMEM(mask.shape, jnp.int32)],
                flops,
                cols, mask, *operands,
            )
        new, send, sq = call(
            step_kernel,
            [BANDED, SEND, jax.ShapeDtypeStruct((Q, 2 * Q), BF)],
            [VMEM] * 3,
            [VMEM] * 7,
            [square],
            flops,
            *operands,
        )
        band = call(
            step_left_kernel, BANDED, VMEM, [VMEM] * 5, [], 0, marks, band, sq, twin, new, alias={4: 0}
        )


def solution(mesh):
    return jax.shard_map(
        on_device,
        mesh=mesh,
        in_specs=(
            P("rows", None, None, None),
            P("rows", None, None, None),
            P("rows", None),
            P("rows", None),
        ),
        out_specs=P("rows", "rep", None, None),
        check_vma=False,
    )
```

```python
import math

import jax
import jax.numpy as jnp
from jax import lax
from jax.experimental import pallas as pl
from jax.experimental.pallas import tpu as pltpu
from jax.sharding import PartitionSpec as P

BAND = 4
STEPS = 2
S = 128
Q = 4 * S
H = 2 * S
TRI = [(p, m) for p in range(4) for m in range(p, 4)]
BF = jnp.bfloat16
F32 = jnp.float32
LEFT, OWN, RIGHT = (0, 1), (2, 3), (4, 5)

VMEM = pl.BlockSpec(memory_space=pltpu.VMEM)
SMEM = pl.BlockSpec(memory_space=pltpu.SMEM)
SQUARE = jax.ShapeDtypeStruct((Q, Q), BF)
CORNER = jax.ShapeDtypeStruct((len(TRI), S, S), BF)
BANDED = jax.ShapeDtypeStruct((Q, 3 * Q), BF)
SEND = jax.ShapeDtypeStruct((6 * S + S // 2, Q), BF)
SUMS = jax.ShapeDtypeStruct((Q, Q), F32)
WIDE = jax.ShapeDtypeStruct((Q, 3 * Q), F32)


def call(kernel, outs, out_specs, in_specs, scratch, flops, *args, room=24, alias=None):
    return pl.pallas_call(
        kernel,
        out_shape=outs,
        in_specs=in_specs,
        out_specs=out_specs,
        scratch_shapes=scratch,
        input_output_aliases=alias or {},
        compiler_params=pltpu.CompilerParams(vmem_limit_bytes=room << 20),
        cost_estimate=pl.CostEstimate(flops=flops, bytes_accessed=4 << 20, transcendentals=0),
    )(*args)


def place(cols_ref, mask_ref, a, s):
    first = lax.axis_index("rows") * 4 - BAND
    core = lax.axis_index("rep")
    k = cols_ref[a, s] - first
    k = jnp.clip(k, 0, 11)
    k = jnp.where(core == 1, 11 - k, k)
    row = jnp.where(core == 1, 3 - a, a)
    t = jnp.where(k < 4, 3 - k, k)
    return mask_ref[a, s] == 1, row, t


def at(index):
    return pl.ds(pl.multiple_of(index * S, S), S)


def eye():
    rows = lax.broadcasted_iota(jnp.int32, (S, S), 0)
    cols = lax.broadcasted_iota(jnp.int32, (S, S), 1)
    return (rows == cols).astype(F32)


def joint_put(joint, index, block):
    if index >= 24:
        col = (index - 24) * 2 * S
        joint[6 * S :, col : col + S] = block[: S // 2]
        joint[6 * S :, col + S : col + 2 * S] = block[S // 2 :]
    else:
        row, col = index // 4 * S, index % 4 * S
        joint[row : row + S, col : col + S] = block


def joint_block(joint, index):
    if index >= 24:
        col = (index - 24) * 2 * S
        return jnp.concatenate([joint[6 * S :, col : col + S], joint[6 * S :, col + S : col + 2 * S]], axis=0)
    row, col = index // 4 * S, index % 4 * S
    return joint[row : row + S, col : col + S]


def joint_send(joint, row, t, block):
    if 4 <= t < 8:
        joint_put(joint, 4 * (3 - row) + 7 - t, block)
    if t >= 8 and (3 - row, 11 - t) in TRI:
        joint_put(joint, 16 + TRI.index((3 - row, 11 - t)), block)


def fill_table(cols, mask, table):
    for i in range(48):
        table[i] = -1
    for a in range(4):
        for s in range(8):
            active, row, t = place(cols, mask, a, s)
            table[jnp.where(active, 12 * row + t, 48)] = s


def source_row(row):
    return jnp.where(lax.axis_index("rep") == 1, 3 - row, row)


def row_block(ref, table, row, t, source=None):
    slot = table[12 * row + t]
    block = ref[row if source is None else source, jnp.maximum(slot, 0)]
    return jnp.where(slot >= 0, block, jnp.zeros_like(block))


def slot_block(ref, table, row, t):
    return row_block(ref, table, row, t, source_row(row))


def x_slot_block(ref, table, diag, row, t):
    block = slot_block(ref, table, row, t)
    return (block.astype(F32) + diag).astype(BF) if t - 4 == row else block


def pack_h_kernel(cols_hbm, mask_hbm, h_hbm, send, table, h_ref, cols, mask, sems):
    pattern = [
        pltpu.make_async_copy(cols_hbm, cols, sems.at[0]),
        pltpu.make_async_copy(mask_hbm, mask, sems.at[1]),
    ]
    rows = [pltpu.make_async_copy(h_hbm.at[source_row(row)], h_ref.at[row], sems.at[2 + row]) for row in range(4)]
    for copy in pattern + rows:
        copy.start()
    for copy in pattern:
        copy.wait()
    fill_table(cols, mask, table)
    for row in range(4):
        rows[row].wait()
        for t in range(4, 12):
            joint_send(send, row, t, row_block(h_ref, table, row, t))


def pack_x_kernel(table, x_ref, xa, xb, marks):
    diag = eye()
    for index, (p, m) in enumerate(TRI):
        xa[index] = slot_block(x_ref, table, 3 - p, 11 - m)
    for row in range(4):
        for m in range(4):
            put(xb, 3 - row, 3 - m, x_slot_block(x_ref, table, diag, row, 4 + m))
    for i in range(48):
        marks[i : i + 1, :] = jnp.full((1, S), jnp.where(table[i] >= 0, 1.0, 0.0), F32)


def spread_mine(get, square_ref):
    square_ref[H:, :H] = jnp.zeros((H, H), BF)
    square_ref[S : 2 * S, :S] = jnp.zeros((S, S), BF)
    square_ref[3 * S :, H : 3 * S] = jnp.zeros((S, S), BF)
    for index, (p, m) in enumerate(TRI):
        square_ref[p * S : (p + 1) * S, m * S : (m + 1) * S] = get(index)


def spread_twin(get, square_ref):
    square_ref[H:, H:] = jnp.zeros((H, H), BF)
    square_ref[S : 2 * S, 3 * S :] = jnp.zeros((S, S), BF)
    square_ref[3 * S :, S:H] = jnp.zeros((S, S), BF)
    for index, (p, m) in enumerate(TRI):
        square_ref[p * S : (p + 1) * S, (3 - m) * S : (4 - m) * S] = get(index)


def tile(ref, i, j):
    return ref[i * H : (i + 1) * H, j * H : (j + 1) * H]


def right_operand(ll, lc, own, rc, rr):
    def get(t, u):
        if t in OWN:
            if (t, u) in ((3, 1), (2, 5)):
                return None
            return own(t - 2, u)
        if t in LEFT:
            if u in LEFT:
                return tile(ll, t, u)
            if u in OWN and (t, u) != (1, 3):
                return tile(lc, t, u - 2)
            return None
        if u in RIGHT:
            return tile(rr, t - 4, u - 4)
        if u in OWN and (t, u) != (5, 2):
            return tile(rc, t - 4, u - 2)
        return None

    return get


def left_tile(ref, r, t):
    if (r, t) in ((1, 1), (0, 5)):
        return None
    return tile(ref, r, t)


def product(left, right, columns, finish):
    for u in columns:
        for r in range(2):
            if (r, u) in ((1, 1), (0, 5)):
                continue
            xs, ys = [], []
            for t in range(6):
                x = left(r, t)
                y = None if x is None else right(t, u)
                if y is not None:
                    xs.append(x)
                    ys.append(y)
            total = None
            if xs:
                x, y = jnp.concatenate(xs, axis=1), jnp.concatenate(ys, axis=0)
                total = jnp.dot(x, y, preferred_element_type=F32)
            finish(r, u, total)


def each_block(table_ref, r, u, total, store):
    for i in range(2):
        for j in range(2):
            row, t = 2 * r + i, 2 * u + j
            block = total[i * S : (i + 1) * S, j * S : (j + 1) * S]
            block = jnp.where(table_ref[12 * row + t : 12 * row + t + 1, :] > 0.0, block, 0.0)
            store(row, t, block)


def put(ref, row, t, block):
    ref[row * S : (row + 1) * S, t * S : (t + 1) * S] = block


def put_tile(ref, i, j, value):
    ref[i * H : (i + 1) * H, j * H : (j + 1) * H] = value


def mine_kernel(table, h_ref, x_ref, joint, xo, part, ho, rc):
    diag = eye()
    for row in range(4):
        for t in range(12):
            put(ho, row, t, row_block(h_ref, table, row, t))
            put(xo, row, t, x_slot_block(x_ref, table, diag, row, t))
    spread_mine(lambda i: joint_block(joint, 16 + i), rc)
    right = right_operand(None, None, lambda r, u: tile(ho, r, u), rc, joint)
    left = lambda r, t: None if t in LEFT else left_tile(xo, r, t)
    product(left, right, range(6), lambda r, u, total: put_tile(part, r, u, total))


def spread_kernel(xa, part, copy, square):
    copy[...] = xa[...]
    spread_mine(lambda i: xa[i], square)


def half_kernel(table, xo, twin, part, half_ref, lc):
    spread_twin(lambda i: joint_block(twin, 16 + i), lc)
    half_ref[H:, H:Q] = jnp.zeros((H, H), BF)
    half_ref[:H, 2 * Q + H :] = jnp.zeros((H, H), BF)
    right = right_operand(twin, lc, None, None, None)

    def keep(r, u, total):
        total = tile(part, r, u) if total is None else total + tile(part, r, u)
        each_block(table, r, u, total, lambda row, t, b: put(half_ref, row, t, b.astype(BF)))

    product(lambda r, t: left_tile(xo, r, t) if t in LEFT else None, right, range(6), keep)


def center_kernel(factor, table, half, xo, xrc, xa2, band, send, xlc):
    spread_twin(lambda i: xa2[i], xlc)
    right = right_operand(None, xlc, lambda r, u: tile(xo, r, u), xrc, None)
    diag = eye()

    def start(r, u, total):
        def store(row, t, block):
            value = -factor * block
            if t - 4 == row:
                value = value + 0.5 * diag
            value = value.astype(BF)
            put(band, row, t, value)
            joint_send(send, row, t, value)

        each_block(table, r, u, total, store)

    product(lambda r, t: left_tile(half, r, t), right, OWN, start)


def side_kernel(factor, table, half, xo, xb, band_in, send_in, band, send, side):
    right = right_operand(None, None, lambda r, u: tile(xo, r, u), None, xb)

    def start(r, u, total):
        def store(row, t, block):
            value = (-factor * block).astype(BF)
            put(band, row, t, value)
            joint_send(send, row, t, value)
            if (3 - row, 11 - t) in TRI:
                side[TRI.index((3 - row, 11 - t))] = value

        each_block(table, r, u, total, store)

    product(lambda r, t: left_tile(half, r, t), right, RIGHT, start)


def mine_squares_kernel(table, band, joint, sq_r, part_l, sums, more, rc):
    spread_mine(lambda i: joint_block(joint, 16 + i), rc)
    sq_r[:H, H:] = jnp.zeros((H, H), BF)
    right = right_operand(None, None, lambda r, u: tile(band, r, u), rc, joint)

    def keep(r, u, total):
        if u in LEFT:
            put_tile(part_l, r, u, total)
        elif u in OWN:
            put_tile(sums, r, u - 2, total)
        else:
            each_block(table, r, u, total, lambda row, t, b: put(sq_r, row, t - 8, b.astype(BF)))

    product(lambda r, t: None if t in LEFT else left_tile(band, r, t), right, RIGHT + OWN + LEFT, keep)

    def square(r, t):
        return None if t not in RIGHT or (r, t) == (0, 5) else tile(sq_r, r, t - 4)

    product(square, right, OWN + RIGHT, lambda r, u, total: put_tile(more, r, u - 2, total))


def late_kernel(columns, table, band, sq_r, part_l, sums, more, twin, lc, sq, finish, after=None):
    spread_twin(lambda i: joint_block(twin, 16 + i), lc)
    right = right_operand(twin, lc, lambda r, u: tile(band, r, u), None, None)

    for half in range(2):

        def only(left, *places):
            return lambda r, t: left(r, t) if r == half and t in places else None

        def keep(r, u, total):
            if r != half:
                return
            total = total + (tile(sums, r, u - 2) if u in OWN else tile(part_l, r, u))
            each_block(table, r, u, total, lambda row, t, b: put(sq, row, t, b.astype(BF)))

        def step(r, u, total):
            if r != half:
                return
            if u not in LEFT:
                total = total + tile(more, r, u - 2)

            def store(row, t, block):
                if u in RIGHT:
                    now = sq_r[row * S : (row + 1) * S, (t - 8) * S : (t - 7) * S]
                else:
                    now = sq[row * S : (row + 1) * S, t * S : (t + 1) * S]
                finish(row, t, (3.0 * now.astype(F32) - 2.0 * block).astype(BF))

            each_block(table, r, u, total, store)

        product(only(lambda r, t: left_tile(band, r, t), *LEFT), right, LEFT + OWN, keep)
        product(only(lambda r, t: left_tile(sq, r, t), *LEFT, *OWN), right, columns, step)
        if after:
            after(half)


def step_kernel(table, band, sq_r, part_l, sums, more, twin, new, send, sq, lc):
    def finish(row, t, value):
        put(new, row, t, value)
        joint_send(send, row, t, value)

    late_kernel(OWN + RIGHT, table, band, sq_r, part_l, sums, more, twin, lc, sq, finish)


def step_left_kernel(table, band, sq, twin, new_in, new):
    new[H:, H:Q] = jnp.zeros((H, H), BF)
    new[:H, 2 * Q + H :] = jnp.zeros((H, H), BF)
    right = right_operand(twin, None, lambda r, u: tile(band, r, u), None, None)

    def step(r, u, total):
        def store(row, t, block):
            now = sq[row * S : (row + 1) * S, t * S : (t + 1) * S]
            put(new, row, t, (3.0 * now.astype(F32) - 2.0 * block).astype(BF))

        each_block(table, r, u, total, store)

    product(lambda r, t: None if t in RIGHT else left_tile(sq, r, t), right, LEFT, step)


def last_kernel(cols_hbm, mask_hbm, table, band, sq_r, part_l, sums, more, twin, out_hbm, *scratch):
    lc, sq, res, out, sems, cols, mask = scratch
    core = lax.axis_index("rep")
    pattern = [
        pltpu.make_async_copy(cols_hbm, cols, sems.at[4]),
        pltpu.make_async_copy(mask_hbm, mask, sems.at[5]),
    ]
    for one in pattern:
        one.start()

    def copy(row):
        return pltpu.make_async_copy(out.at[row], out_hbm.at[source_row(row)], sems.at[row])

    def after(half):
        if half == 0:
            for one in pattern:
                one.wait()
        for row in (2 * half, 2 * half + 1):
            for s in range(4):
                active, unused, t = place(cols, mask, source_row(row), core * 4 + s)
                block = res[row * S : (row + 1) * S, at(t)]
                out[row, s] = jnp.where(active, block, jnp.zeros_like(block))
            copy(row).start()

    late_kernel(
        LEFT + OWN + RIGHT, table, band, sq_r, part_l, sums, more, twin, lc, sq, lambda row, t, value: put(res, row, t, value), after
    )
    for row in range(4):
        copy(row).wait()


def join_kernel(band, side, out):
    out[:, Q:] = band[:, Q:]
    out[:H, 2 * Q + H :] = jnp.zeros((H, H), BF)
    spread_twin(lambda i: side[i], out.at[:, :Q])


def on_device(hamiltonian, x_correction, cols, mask):
    n = lax.axis_size("rows")
    factor = 0.6 / math.sqrt(cols.shape[1] * hamiltonian.shape[-1])
    outward = [(2 * i, 2 * i + 3) for i in range(n - 1)] + [(2 * i + 1, 2 * i - 2) for i in range(1, n)]

    def link(x):
        return lax.ppermute(x, ("rows", "rep"), outward)

    def swap(x):
        return lax.ppermute(x, "rep", [(0, 1), (1, 0)])

    square = pltpu.VMEM((Q, Q), BF)
    flops = 1 << 29
    hbm = pl.BlockSpec(memory_space=pltpu.HBM)

    index_table = pltpu.SMEM((49,), jnp.int32)
    h_send, table, h_rows = call(
        pack_h_kernel,
        [SEND, index_table, jax.ShapeDtypeStruct(hamiltonian.shape, BF)],
        [VMEM, SMEM, VMEM],
        [hbm] * 3,
        [
            pltpu.SMEM(cols.shape, jnp.int32),
            pltpu.SMEM(mask.shape, jnp.int32),
            pltpu.SemaphoreType.DMA((6,)),
        ],
        flops,
        *(pltpu.with_memory_space_constraint(x, pltpu.HBM) for x in (cols, mask, hamiltonian)),
    )
    h_halo = link(h_send)
    xa, xb, marks = call(
        pack_x_kernel,
        [CORNER, SQUARE, jax.ShapeDtypeStruct((48, S), F32)],
        [VMEM] * 3,
        [SMEM, VMEM],
        [],
        0,
        table, x_correction,
    )
    xa_halo = link(xa)
    xb_halo = link(xb)
    h_twin = swap(h_halo)
    xo, part = call(
        mine_kernel,
        [BANDED, WIDE],
        [VMEM] * 2,
        [SMEM] + [VMEM] * 3,
        [pltpu.VMEM((Q, 3 * Q), BF), square],
        64 * flops,
        table, h_rows, x_correction, h_halo,
    )
    xa_copy, x_corner = call(spread_kernel, [CORNER, SQUARE], [VMEM] * 2, [VMEM] * 2, [], 0, xa_halo, part)
    xa_twin = swap(xa_copy)
    half = call(half_kernel, BANDED, VMEM, [VMEM] + [VMEM] * 3, [square], 16 * flops, marks, xo, h_twin, part)
    band, send = call(
        lambda *refs: center_kernel(factor, *refs),
        [BANDED, SEND],
        [VMEM] * 2,
        [VMEM] * 5,
        [square],
        flops,
        marks, half, xo, x_corner, xa_twin,
    )
    band, send, side = call(
        lambda *refs: side_kernel(factor, *refs),
        [BANDED, SEND, CORNER],
        [VMEM] * 3,
        [VMEM] * 6,
        [],
        flops,
        marks, half, xo, xb_halo, band, send,
        alias={4: 0, 5: 1},
    )
    halo = link(send)
    band = call(join_kernel, BANDED, VMEM, [VMEM] * 2, [], 0, band, swap(side))
    for step in range(STEPS):
        if step > 0:
            halo = link(send)
        twin = swap(halo)
        sq_r, part_l, sums, more = call(
            mine_squares_kernel,
            [SQUARE, SUMS, SUMS, jax.ShapeDtypeStruct((Q, 2 * Q), F32)],
            [VMEM] * 4,
            [VMEM] + [VMEM] * 2,
            [square],
            64 * flops,
            marks, band, halo,
        )
        operands = (marks, band, sq_r, part_l, sums, more, twin)
        if step + 1 == STEPS:
            return call(
                last_kernel,
                jax.ShapeDtypeStruct((4, 4, S, S), BF),
                hbm,
                [hbm] * 2 + [VMEM] * 7,
                [square, pltpu.VMEM((Q, 2 * Q), BF)]
                + [pltpu.VMEM((Q, 3 * Q), BF), pltpu.VMEM((4, 4, S, S), BF), pltpu.SemaphoreType.DMA((6,))]
                + [pltpu.SMEM(cols.shape, jnp.int32), pltpu.SMEM(mask.shape, jnp.int32)],
                flops,
                cols, mask, *operands,
            )
        new, send, sq = call(
            step_kernel,
            [BANDED, SEND, jax.ShapeDtypeStruct((Q, 2 * Q), BF)],
            [VMEM] * 3,
            [VMEM] * 7,
            [square],
            flops,
            *operands,
        )
        band = call(
            step_left_kernel, BANDED, VMEM, [VMEM] * 5, [], 0, marks, band, sq, twin, new, alias={4: 0}
        )


def solution(mesh):
    return jax.shard_map(
        on_device,
        mesh=mesh,
        in_specs=(
            P("rows", None, None, None),
            P("rows", None, None, None),
            P("rows", None),
            P("rows", None),
        ),
        out_specs=P("rows", "rep", None, None),
        check_vma=False,
    )
```

```python
import math

import jax
import jax.numpy as jnp
from jax import lax
from jax.experimental import pallas as pl
from jax.experimental.pallas import tpu as pltpu
from jax.sharding import PartitionSpec as P

BAND = 4
STEPS = 2
S = 128
Q = 4 * S
H = 2 * S
TRI = [(p, m) for p in range(4) for m in range(p, 4)]
BF = jnp.bfloat16
F32 = jnp.float32
LEFT, OWN, RIGHT = (0, 1), (2, 3), (4, 5)

VMEM = pl.BlockSpec(memory_space=pltpu.VMEM)
SMEM = pl.BlockSpec(memory_space=pltpu.SMEM)
SQUARE = jax.ShapeDtypeStruct((Q, Q), BF)
CORNER = jax.ShapeDtypeStruct((len(TRI), S, S), BF)
BANDED = jax.ShapeDtypeStruct((Q, 3 * Q), BF)
SEND = jax.ShapeDtypeStruct((6 * S + S // 2, Q), BF)
SUMS = jax.ShapeDtypeStruct((Q, Q), F32)
WIDE = jax.ShapeDtypeStruct((Q, 3 * Q), F32)


def call(kernel, outs, out_specs, in_specs, scratch, flops, *args, room=24, alias=None):
    return pl.pallas_call(
        kernel,
        out_shape=outs,
        in_specs=in_specs,
        out_specs=out_specs,
        scratch_shapes=scratch,
        input_output_aliases=alias or {},
        compiler_params=pltpu.CompilerParams(vmem_limit_bytes=room << 20),
        cost_estimate=pl.CostEstimate(flops=flops, bytes_accessed=4 << 20, transcendentals=0),
    )(*args)


def place(cols_ref, mask_ref, a, s):
    first = lax.axis_index("rows") * 4 - BAND
    core = lax.axis_index("rep")
    k = cols_ref[a, s] - first
    k = jnp.clip(k, 0, 11)
    k = jnp.where(core == 1, 11 - k, k)
    row = jnp.where(core == 1, 3 - a, a)
    t = jnp.where(k < 4, 3 - k, k)
    return mask_ref[a, s] == 1, row, t


def at(index):
    return pl.ds(pl.multiple_of(index * S, S), S)


def eye():
    rows = lax.broadcasted_iota(jnp.int32, (S, S), 0)
    cols = lax.broadcasted_iota(jnp.int32, (S, S), 1)
    return (rows == cols).astype(F32)


def joint_put(joint, index, block):
    if index >= 24:
        col = (index - 24) * 2 * S
        joint[6 * S :, col : col + S] = block[: S // 2]
        joint[6 * S :, col + S : col + 2 * S] = block[S // 2 :]
    else:
        row, col = index // 4 * S, index % 4 * S
        joint[row : row + S, col : col + S] = block


def joint_block(joint, index):
    if index >= 24:
        col = (index - 24) * 2 * S
        return jnp.concatenate([joint[6 * S :, col : col + S], joint[6 * S :, col + S : col + 2 * S]], axis=0)
    row, col = index // 4 * S, index % 4 * S
    return joint[row : row + S, col : col + S]


def joint_send(joint, row, t, block):
    if 4 <= t < 8:
        joint_put(joint, 4 * (3 - row) + 7 - t, block)
    if t >= 8 and (3 - row, 11 - t) in TRI:
        joint_put(joint, 16 + TRI.index((3 - row, 11 - t)), block)


def fill_table(cols, mask, table):
    for i in range(48):
        table[i] = -1
    for a in range(4):
        for s in range(8):
            active, row, t = place(cols, mask, a, s)
            table[jnp.where(active, 12 * row + t, 48)] = s
            table[49 + 8 * row + s] = jnp.where(active, t, -1)


def source_row(row):
    return jnp.where(lax.axis_index("rep") == 1, 3 - row, row)


def row_block(ref, table, row, t, source=None):
    slot = table[12 * row + t]
    block = ref[row if source is None else source, jnp.maximum(slot, 0)]
    return jnp.where(slot >= 0, block, jnp.zeros_like(block))


def slot_block(ref, table, row, t):
    return row_block(ref, table, row, t, source_row(row))


def x_slot_block(ref, table, diag, row, t):
    block = slot_block(ref, table, row, t)
    return (block.astype(F32) + diag).astype(BF) if t - 4 == row else block


def pack_h_kernel(cols_hbm, mask_hbm, h_hbm, send, table, h_ref, cols, mask, sems):
    pattern = [
        pltpu.make_async_copy(cols_hbm, cols, sems.at[0]),
        pltpu.make_async_copy(mask_hbm, mask, sems.at[1]),
    ]
    rows = [pltpu.make_async_copy(h_hbm.at[source_row(row)], h_ref.at[row], sems.at[2 + row]) for row in range(4)]
    for copy in pattern + rows:
        copy.start()
    for copy in pattern:
        copy.wait()
    fill_table(cols, mask, table)
    for row in range(4):
        rows[row].wait()
        for t in range(4, 12):
            joint_send(send, row, t, row_block(h_ref, table, row, t))


def pack_x_kernel(table, x_ref, xa, xb, marks):
    diag = eye()
    for index, (p, m) in enumerate(TRI):
        xa[index] = slot_block(x_ref, table, 3 - p, 11 - m)
    for row in range(4):
        for m in range(4):
            put(xb, 3 - row, 3 - m, x_slot_block(x_ref, table, diag, row, 4 + m))
    for i in range(48):
        marks[i : i + 1, :] = jnp.full((1, S), jnp.where(table[i] >= 0, 1.0, 0.0), F32)


def spread_mine(get, square_ref):
    square_ref[H:, :H] = jnp.zeros((H, H), BF)
    square_ref[S : 2 * S, :S] = jnp.zeros((S, S), BF)
    square_ref[3 * S :, H : 3 * S] = jnp.zeros((S, S), BF)
    for index, (p, m) in enumerate(TRI):
        square_ref[p * S : (p + 1) * S, m * S : (m + 1) * S] = get(index)


def spread_twin(get, square_ref):
    square_ref[H:, H:] = jnp.zeros((H, H), BF)
    square_ref[S : 2 * S, 3 * S :] = jnp.zeros((S, S), BF)
    square_ref[3 * S :, S:H] = jnp.zeros((S, S), BF)
    for index, (p, m) in enumerate(TRI):
        square_ref[p * S : (p + 1) * S, (3 - m) * S : (4 - m) * S] = get(index)


def tile(ref, i, j):
    return ref[i * H : (i + 1) * H, j * H : (j + 1) * H]


def right_operand(ll, lc, own, rc, rr):
    def get(t, u):
        if t in OWN:
            if (t, u) in ((3, 1), (2, 5)):
                return None
            return own(t - 2, u)
        if t in LEFT:
            if u in LEFT:
                return tile(ll, t, u)
            if u in OWN and (t, u) != (1, 3):
                return tile(lc, t, u - 2)
            return None
        if u in RIGHT:
            return tile(rr, t - 4, u - 4)
        if u in OWN and (t, u) != (5, 2):
            return tile(rc, t - 4, u - 2)
        return None

    return get


def left_tile(ref, r, t):
    if (r, t) in ((1, 1), (0, 5)):
        return None
    return tile(ref, r, t)


def product(left, right, columns, finish):
    for u in columns:
        for r in range(2):
            if (r, u) in ((1, 1), (0, 5)):
                continue
            xs, ys = [], []
            for t in range(6):
                x = left(r, t)
                y = None if x is None else right(t, u)
                if y is not None:
                    xs.append(x)
                    ys.append(y)
            total = None
            if xs:
                x, y = jnp.concatenate(xs, axis=1), jnp.concatenate(ys, axis=0)
                total = jnp.dot(x, y, preferred_element_type=F32)
            finish(r, u, total)


def each_block(table_ref, r, u, total, store):
    for i in range(2):
        for j in range(2):
            row, t = 2 * r + i, 2 * u + j
            block = total[i * S : (i + 1) * S, j * S : (j + 1) * S]
            block = jnp.where(table_ref[12 * row + t : 12 * row + t + 1, :] > 0.0, block, 0.0)
            store(row, t, block)


def put(ref, row, t, block):
    ref[row * S : (row + 1) * S, t * S : (t + 1) * S] = block


def put_tile(ref, i, j, value):
    ref[i * H : (i + 1) * H, j * H : (j + 1) * H] = value


def mine_kernel(table, h_ref, x_ref, joint, xo, part, ho, rc):
    diag = eye()
    for row in range(4):
        for t in range(12):
            put(ho, row, t, row_block(h_ref, table, row, t))
            put(xo, row, t, x_slot_block(x_ref, table, diag, row, t))
    spread_mine(lambda i: joint_block(joint, 16 + i), rc)
    right = right_operand(None, None, lambda r, u: tile(ho, r, u), rc, joint)
    left = lambda r, t: None if t in LEFT else left_tile(xo, r, t)
    product(left, right, range(6), lambda r, u, total: put_tile(part, r, u, total))


def spread_kernel(xa, part, copy, square):
    copy[...] = xa[...]
    spread_mine(lambda i: xa[i], square)


def half_kernel(table, xo, twin, part, half_ref, lc):
    spread_twin(lambda i: joint_block(twin, 16 + i), lc)
    half_ref[H:, H:Q] = jnp.zeros((H, H), BF)
    half_ref[:H, 2 * Q + H :] = jnp.zeros((H, H), BF)
    right = right_operand(twin, lc, None, None, None)

    def keep(r, u, total):
        total = tile(part, r, u) if total is None else total + tile(part, r, u)
        each_block(table, r, u, total, lambda row, t, b: put(half_ref, row, t, b.astype(BF)))

    product(lambda r, t: left_tile(xo, r, t) if t in LEFT else None, right, range(6), keep)


def center_kernel(factor, table, half, xo, xrc, xa2, band, send, xlc):
    spread_twin(lambda i: xa2[i], xlc)
    right = right_operand(None, xlc, lambda r, u: tile(xo, r, u), xrc, None)
    diag = eye()

    def start(r, u, total):
        def store(row, t, block):
            value = -factor * block
            if t - 4 == row:
                value = value + 0.5 * diag
            value = value.astype(BF)
            put(band, row, t, value)
            joint_send(send, row, t, value)

        each_block(table, r, u, total, store)

    product(lambda r, t: left_tile(half, r, t), right, OWN, start)


def side_kernel(factor, table, half, xo, xb, band_in, send_in, band, send, side):
    right = right_operand(None, None, lambda r, u: tile(xo, r, u), None, xb)

    def start(r, u, total):
        def store(row, t, block):
            value = (-factor * block).astype(BF)
            put(band, row, t, value)
            joint_send(send, row, t, value)
            if (3 - row, 11 - t) in TRI:
                side[TRI.index((3 - row, 11 - t))] = value

        each_block(table, r, u, total, store)

    product(lambda r, t: left_tile(half, r, t), right, RIGHT, start)


def mine_squares_kernel(table, band, joint, sq_r, part_l, sums, more, rc):
    spread_mine(lambda i: joint_block(joint, 16 + i), rc)
    sq_r[:H, H:] = jnp.zeros((H, H), BF)
    right = right_operand(None, None, lambda r, u: tile(band, r, u), rc, joint)

    def keep(r, u, total):
        if u in LEFT:
            put_tile(part_l, r, u, total)
        elif u in OWN:
            put_tile(sums, r, u - 2, total)
        else:
            each_block(table, r, u, total, lambda row, t, b: put(sq_r, row, t - 8, b.astype(BF)))

    product(lambda r, t: None if t in LEFT else left_tile(band, r, t), right, RIGHT + OWN + LEFT, keep)

    def square(r, t):
        return None if t not in RIGHT or (r, t) == (0, 5) else tile(sq_r, r, t - 4)

    product(square, right, OWN + RIGHT, lambda r, u, total: put_tile(more, r, u - 2, total))


def late_kernel(columns, table, band, sq_r, part_l, sums, more, twin, lc, sq, finish, after=None):
    spread_twin(lambda i: joint_block(twin, 16 + i), lc)
    right = right_operand(twin, lc, lambda r, u: tile(band, r, u), None, None)

    def keep(r, u, total):
        total = total + (tile(sums, r, u - 2) if u in OWN else tile(part_l, r, u))
        each_block(table, r, u, total, lambda row, t, b: put(sq, row, t, b.astype(BF)))

    def step(r, u, total):
        if u not in LEFT:
            total = total + tile(more, r, u - 2)

        def store(row, t, block):
            if u in RIGHT:
                now = sq_r[row * S : (row + 1) * S, (t - 8) * S : (t - 7) * S]
            else:
                now = sq[row * S : (row + 1) * S, t * S : (t + 1) * S]
            finish(row, t, (3.0 * now.astype(F32) - 2.0 * block).astype(BF))

        each_block(table, r, u, total, store)

    product(lambda r, t: left_tile(band, r, t) if t in LEFT else None, right, LEFT + OWN, keep)
    product(lambda r, t: None if t in RIGHT else left_tile(sq, r, t), right, columns, step)
    if after:
        after(0)
        after(1)


def step_kernel(table, band, sq_r, part_l, sums, more, twin, new, send, sq, lc):
    def finish(row, t, value):
        put(new, row, t, value)
        joint_send(send, row, t, value)

    late_kernel(OWN + RIGHT, table, band, sq_r, part_l, sums, more, twin, lc, sq, finish)


def step_left_kernel(table, band, sq, twin, new_in, new):
    new[H:, H:Q] = jnp.zeros((H, H), BF)
    new[:H, 2 * Q + H :] = jnp.zeros((H, H), BF)
    right = right_operand(twin, None, lambda r, u: tile(band, r, u), None, None)

    def step(r, u, total):
        def store(row, t, block):
            now = sq[row * S : (row + 1) * S, t * S : (t + 1) * S]
            put(new, row, t, (3.0 * now.astype(F32) - 2.0 * block).astype(BF))

        each_block(table, r, u, total, store)

    product(lambda r, t: None if t in RIGHT else left_tile(sq, r, t), right, LEFT, step)


def last_kernel(index, table, band, sq_r, part_l, sums, more, twin, out_hbm, *scratch):
    lc, sq, res, out, sems = scratch
    core = lax.axis_index("rep")

    def copy(row):
        return pltpu.make_async_copy(out.at[row], out_hbm.at[source_row(row)], sems.at[row])

    def after(half):
        for row in (2 * half, 2 * half + 1):
            for s in range(4):
                t = index[49 + 8 * row + core * 4 + s]
                block = res[row * S : (row + 1) * S, at(jnp.maximum(t, 0))]
                out[row, s] = jnp.where(t >= 0, block, jnp.zeros_like(block))
            copy(row).start()

    late_kernel(
        LEFT + OWN + RIGHT, table, band, sq_r, part_l, sums, more, twin, lc, sq,
        lambda row, t, value: put(res, row, t, value), after,
    )
    for row in range(4):
        copy(row).wait()


def join_kernel(band, side, out):
    out[:, Q:] = band[:, Q:]
    out[:H, 2 * Q + H :] = jnp.zeros((H, H), BF)
    spread_twin(lambda i: side[i], out.at[:, :Q])


def on_device(hamiltonian, x_correction, cols, mask):
    n = lax.axis_size("rows")
    factor = 0.6 / math.sqrt(cols.shape[1] * hamiltonian.shape[-1])
    outward = [(2 * i, 2 * i + 3) for i in range(n - 1)] + [(2 * i + 1, 2 * i - 2) for i in range(1, n)]

    def link(x):
        return lax.ppermute(x, ("rows", "rep"), outward)

    def swap(x):
        return lax.ppermute(x, "rep", [(0, 1), (1, 0)])

    square = pltpu.VMEM((Q, Q), BF)
    flops = 1 << 29
    hbm = pl.BlockSpec(memory_space=pltpu.HBM)

    index_table = pltpu.SMEM((81,), jnp.int32)
    h_send, table, h_rows = call(
        pack_h_kernel,
        [SEND, index_table, jax.ShapeDtypeStruct(hamiltonian.shape, BF)],
        [VMEM, SMEM, VMEM],
        [hbm] * 3,
        [
            pltpu.SMEM(cols.shape, jnp.int32),
            pltpu.SMEM(mask.shape, jnp.int32),
            pltpu.SemaphoreType.DMA((6,)),
        ],
        flops,
        *(pltpu.with_memory_space_constraint(x, pltpu.HBM) for x in (cols, mask, hamiltonian)),
    )
    h_halo = link(h_send)
    xa, xb, marks = call(
        pack_x_kernel,
        [CORNER, SQUARE, jax.ShapeDtypeStruct((48, S), F32)],
        [VMEM] * 3,
        [SMEM, VMEM],
        [],
        0,
        table, x_correction,
    )
    xa_halo = link(xa)
    xb_halo = link(xb)
    h_twin = swap(h_halo)
    xo, part = call(
        mine_kernel,
        [BANDED, WIDE],
        [VMEM] * 2,
        [SMEM] + [VMEM] * 3,
        [pltpu.VMEM((Q, 3 * Q), BF), square],
        64 * flops,
        table, h_rows, x_correction, h_halo,
    )
    xa_copy, x_corner = call(spread_kernel, [CORNER, SQUARE], [VMEM] * 2, [VMEM] * 2, [], 0, xa_halo, part)
    xa_twin = swap(xa_copy)
    half = call(half_kernel, BANDED, VMEM, [VMEM] + [VMEM] * 3, [square], 16 * flops, marks, xo, h_twin, part)
    band, send = call(
        lambda *refs: center_kernel(factor, *refs),
        [BANDED, SEND],
        [VMEM] * 2,
        [VMEM] * 5,
        [square],
        flops,
        marks, half, xo, x_corner, xa_twin,
    )
    band, send, side = call(
        lambda *refs: side_kernel(factor, *refs),
        [BANDED, SEND, CORNER],
        [VMEM] * 3,
        [VMEM] * 6,
        [],
        flops,
        marks, half, xo, xb_halo, band, send,
        alias={4: 0, 5: 1},
    )
    halo = link(send)
    band = call(join_kernel, BANDED, VMEM, [VMEM] * 2, [], 0, band, swap(side))
    for step in range(STEPS):
        if step > 0:
            halo = link(send)
        twin = swap(halo)
        sq_r, part_l, sums, more = call(
            mine_squares_kernel,
            [SQUARE, SUMS, SUMS, jax.ShapeDtypeStruct((Q, 2 * Q), F32)],
            [VMEM] * 4,
            [VMEM] + [VMEM] * 2,
            [square],
            64 * flops,
            marks, band, halo,
        )
        operands = (marks, band, sq_r, part_l, sums, more, twin)
        if step + 1 == STEPS:
            return call(
                last_kernel,
                jax.ShapeDtypeStruct((4, 4, S, S), BF),
                hbm,
                [SMEM] + [VMEM] * 7,
                [square, pltpu.VMEM((Q, 2 * Q), BF)]
                + [pltpu.VMEM((Q, 3 * Q), BF), pltpu.VMEM((4, 4, S, S), BF), pltpu.SemaphoreType.DMA((4,))],
                flops,
                table, *operands,
            )
        new, send, sq = call(
            step_kernel,
            [BANDED, SEND, jax.ShapeDtypeStruct((Q, 2 * Q), BF)],
            [VMEM] * 3,
            [VMEM] * 7,
            [square],
            flops,
            *operands,
        )
        band = call(
            step_left_kernel, BANDED, VMEM, [VMEM] * 5, [], 0, marks, band, sq, twin, new, alias={4: 0}
        )


def solution(mesh):
    return jax.shard_map(
        on_device,
        mesh=mesh,
        in_specs=(
            P("rows", None, None, None),
            P("rows", None, None, None),
            P("rows", None),
            P("rows", None),
        ),
        out_specs=P("rows", "rep", None, None),
        check_vma=False,
    )
```

```python
import math

import jax
import jax.numpy as jnp
from jax import lax
from jax.experimental import pallas as pl
from jax.experimental.pallas import tpu as pltpu
from jax.sharding import PartitionSpec as P

BAND = 4
STEPS = 2
S = 128
Q = 4 * S
H = 2 * S
TRI = [(p, m) for p in range(4) for m in range(p, 4)]
BF = jnp.bfloat16
F32 = jnp.float32
LEFT, OWN, RIGHT = (0, 1), (2, 3), (4, 5)

VMEM = pl.BlockSpec(memory_space=pltpu.VMEM)
SMEM = pl.BlockSpec(memory_space=pltpu.SMEM)
SQUARE = jax.ShapeDtypeStruct((Q, Q), BF)
CORNER = jax.ShapeDtypeStruct((len(TRI), S, S), BF)
BANDED = jax.ShapeDtypeStruct((Q, 3 * Q), BF)
SEND = jax.ShapeDtypeStruct((6 * S + S // 2, Q), BF)
SUMS = jax.ShapeDtypeStruct((Q, Q), F32)
WIDE = jax.ShapeDtypeStruct((Q, 3 * Q), F32)


def call(kernel, outs, out_specs, in_specs, scratch, flops, *args, room=24, alias=None):
    return pl.pallas_call(
        kernel,
        out_shape=outs,
        in_specs=in_specs,
        out_specs=out_specs,
        scratch_shapes=scratch,
        input_output_aliases=alias or {},
        compiler_params=pltpu.CompilerParams(vmem_limit_bytes=room << 20),
        cost_estimate=pl.CostEstimate(flops=flops, bytes_accessed=4 << 20, transcendentals=0),
    )(*args)


def place(cols_ref, mask_ref, a, s):
    first = lax.axis_index("rows") * 4 - BAND
    core = lax.axis_index("rep")
    k = cols_ref[a, s] - first
    k = jnp.clip(k, 0, 11)
    k = jnp.where(core == 0, 11 - k, k)
    row = jnp.where(core == 0, 3 - a, a)
    t = jnp.where(k < 4, 3 - k, k)
    return mask_ref[a, s] == 1, row, t


def at(index):
    return pl.ds(pl.multiple_of(index * S, S), S)


def eye():
    rows = lax.broadcasted_iota(jnp.int32, (S, S), 0)
    cols = lax.broadcasted_iota(jnp.int32, (S, S), 1)
    return (rows == cols).astype(F32)


def joint_put(joint, index, block):
    if index >= 24:
        col = (index - 24) * 2 * S
        joint[6 * S :, col : col + S] = block[: S // 2]
        joint[6 * S :, col + S : col + 2 * S] = block[S // 2 :]
    else:
        row, col = index // 4 * S, index % 4 * S
        joint[row : row + S, col : col + S] = block


def joint_block(joint, index):
    if index >= 24:
        col = (index - 24) * 2 * S
        return jnp.concatenate([joint[6 * S :, col : col + S], joint[6 * S :, col + S : col + 2 * S]], axis=0)
    row, col = index // 4 * S, index % 4 * S
    return joint[row : row + S, col : col + S]


def joint_send(joint, row, t, block):
    if 4 <= t < 8:
        joint_put(joint, 4 * (3 - row) + 7 - t, block)
    if t >= 8 and (3 - row, 11 - t) in TRI:
        joint_put(joint, 16 + TRI.index((3 - row, 11 - t)), block)


def fill_table(cols, mask, table):
    for i in range(48):
        table[i] = -1
    for a in range(4):
        for s in range(8):
            active, row, t = place(cols, mask, a, s)
            table[jnp.where(active, 12 * row + t, 48)] = s
            table[49 + 8 * row + s] = jnp.where(active, t, -1)


def source_row(row):
    return jnp.where(lax.axis_index("rep") == 0, 3 - row, row)


def row_block(ref, table, row, t, source=None):
    slot = table[12 * row + t]
    block = ref[row if source is None else source, jnp.maximum(slot, 0)]
    return jnp.where(slot >= 0, block, jnp.zeros_like(block))


def slot_block(ref, table, row, t):
    return row_block(ref, table, row, t, source_row(row))


def x_slot_block(ref, table, diag, row, t):
    block = slot_block(ref, table, row, t)
    return (block.astype(F32) + diag).astype(BF) if t - 4 == row else block


def pack_h_kernel(cols_hbm, mask_hbm, h_hbm, send, table, h_ref, cols, mask, sems):
    pattern = [
        pltpu.make_async_copy(cols_hbm, cols, sems.at[0]),
        pltpu.make_async_copy(mask_hbm, mask, sems.at[1]),
    ]
    rows = [pltpu.make_async_copy(h_hbm.at[source_row(row)], h_ref.at[row], sems.at[2 + row]) for row in range(4)]
    for copy in pattern + rows:
        copy.start()
    for copy in pattern:
        copy.wait()
    fill_table(cols, mask, table)
    for row in range(4):
        rows[row].wait()
        for t in range(4, 12):
            joint_send(send, row, t, row_block(h_ref, table, row, t))


def pack_x_kernel(table, x_ref, xa, xb, marks):
    diag = eye()
    for index, (p, m) in enumerate(TRI):
        xa[index] = slot_block(x_ref, table, 3 - p, 11 - m)
    for row in range(4):
        for m in range(4):
            put(xb, 3 - row, 3 - m, x_slot_block(x_ref, table, diag, row, 4 + m))
    for i in range(48):
        marks[i : i + 1, :] = jnp.full((1, S), jnp.where(table[i] >= 0, 1.0, 0.0), F32)


def spread_mine(get, square_ref):
    square_ref[H:, :H] = jnp.zeros((H, H), BF)
    square_ref[S : 2 * S, :S] = jnp.zeros((S, S), BF)
    square_ref[3 * S :, H : 3 * S] = jnp.zeros((S, S), BF)
    for index, (p, m) in enumerate(TRI):
        square_ref[p * S : (p + 1) * S, m * S : (m + 1) * S] = get(index)


def spread_twin(get, square_ref):
    square_ref[H:, H:] = jnp.zeros((H, H), BF)
    square_ref[S : 2 * S, 3 * S :] = jnp.zeros((S, S), BF)
    square_ref[3 * S :, S:H] = jnp.zeros((S, S), BF)
    for index, (p, m) in enumerate(TRI):
        square_ref[p * S : (p + 1) * S, (3 - m) * S : (4 - m) * S] = get(index)


def tile(ref, i, j):
    return ref[i * H : (i + 1) * H, j * H : (j + 1) * H]


def right_operand(ll, lc, own, rc, rr):
    def get(t, u):
        if t in OWN:
            if (t, u) in ((3, 1), (2, 5)):
                return None
            return own(t - 2, u)
        if t in LEFT:
            if u in LEFT:
                return tile(ll, t, u)
            if u in OWN and (t, u) != (1, 3):
                return tile(lc, t, u - 2)
            return None
        if u in RIGHT:
            return tile(rr, t - 4, u - 4)
        if u in OWN and (t, u) != (5, 2):
            return tile(rc, t - 4, u - 2)
        return None

    return get


def left_tile(ref, r, t):
    if (r, t) in ((1, 1), (0, 5)):
        return None
    return tile(ref, r, t)


def product(left, right, columns, finish):
    for u in columns:
        for r in range(2):
            if (r, u) in ((1, 1), (0, 5)):
                continue
            xs, ys = [], []
            for t in range(6):
                x = left(r, t)
                y = None if x is None else right(t, u)
                if y is not None:
                    xs.append(x)
                    ys.append(y)
            total = None
            if xs:
                x, y = jnp.concatenate(xs, axis=1), jnp.concatenate(ys, axis=0)
                total = jnp.dot(x, y, preferred_element_type=F32)
            finish(r, u, total)


def each_block(table_ref, r, u, total, store):
    for i in range(2):
        for j in range(2):
            row, t = 2 * r + i, 2 * u + j
            block = total[i * S : (i + 1) * S, j * S : (j + 1) * S]
            block = jnp.where(table_ref[12 * row + t : 12 * row + t + 1, :] > 0.0, block, 0.0)
            store(row, t, block)


def put(ref, row, t, block):
    ref[row * S : (row + 1) * S, t * S : (t + 1) * S] = block


def put_tile(ref, i, j, value):
    ref[i * H : (i + 1) * H, j * H : (j + 1) * H] = value


def mine_kernel(table, h_ref, x_ref, joint, xo, part, ho, rc):
    diag = eye()
    for row in range(4):
        for t in range(12):
            put(ho, row, t, row_block(h_ref, table, row, t))
            put(xo, row, t, x_slot_block(x_ref, table, diag, row, t))
    spread_mine(lambda i: joint_block(joint, 16 + i), rc)
    right = right_operand(None, None, lambda r, u: tile(ho, r, u), rc, joint)
    left = lambda r, t: None if t in LEFT else left_tile(xo, r, t)
    product(left, right, range(6), lambda r, u, total: put_tile(part, r, u, total))


def spread_kernel(xa, part, copy, square):
    copy[...] = xa[...]
    spread_mine(lambda i: xa[i], square)


def half_kernel(table, xo, twin, part, half_ref, lc):
    spread_twin(lambda i: joint_block(twin, 16 + i), lc)
    half_ref[H:, H:Q] = jnp.zeros((H, H), BF)
    half_ref[:H, 2 * Q + H :] = jnp.zeros((H, H), BF)
    right = right_operand(twin, lc, None, None, None)

    def keep(r, u, total):
        total = tile(part, r, u) if total is None else total + tile(part, r, u)
        each_block(table, r, u, total, lambda row, t, b: put(half_ref, row, t, b.astype(BF)))

    product(lambda r, t: left_tile(xo, r, t) if t in LEFT else None, right, range(6), keep)


def center_kernel(factor, table, half, xo, xrc, xa2, band, send, xlc):
    spread_twin(lambda i: xa2[i], xlc)
    right = right_operand(None, xlc, lambda r, u: tile(xo, r, u), xrc, None)
    diag = eye()

    def start(r, u, total):
        def store(row, t, block):
            value = -factor * block
            if t - 4 == row:
                value = value + 0.5 * diag
            value = value.astype(BF)
            put(band, row, t, value)
            joint_send(send, row, t, value)

        each_block(table, r, u, total, store)

    product(lambda r, t: left_tile(half, r, t), right, OWN, start)


def side_kernel(factor, table, half, xo, xb, band_in, send_in, band, send, side):
    right = right_operand(None, None, lambda r, u: tile(xo, r, u), None, xb)

    def start(r, u, total):
        def store(row, t, block):
            value = (-factor * block).astype(BF)
            put(band, row, t, value)
            joint_send(send, row, t, value)
            if (3 - row, 11 - t) in TRI:
                side[TRI.index((3 - row, 11 - t))] = value

        each_block(table, r, u, total, store)

    product(lambda r, t: left_tile(half, r, t), right, RIGHT, start)


def mine_squares_kernel(table, band, joint, sq_r, part_l, sums, more, rc):
    spread_mine(lambda i: joint_block(joint, 16 + i), rc)
    sq_r[:H, H:] = jnp.zeros((H, H), BF)
    right = right_operand(None, None, lambda r, u: tile(band, r, u), rc, joint)

    def keep(r, u, total):
        if u in LEFT:
            put_tile(part_l, r, u, total)
        elif u in OWN:
            put_tile(sums, r, u - 2, total)
        else:
            each_block(table, r, u, total, lambda row, t, b: put(sq_r, row, t - 8, b.astype(BF)))

    product(lambda r, t: None if t in LEFT else left_tile(band, r, t), right, RIGHT + OWN + LEFT, keep)

    def square(r, t):
        return None if t not in RIGHT or (r, t) == (0, 5) else tile(sq_r, r, t - 4)

    product(square, right, OWN + RIGHT, lambda r, u, total: put_tile(more, r, u - 2, total))


def late_kernel(columns, table, band, sq_r, part_l, sums, more, twin, lc, sq, finish, after=None):
    spread_twin(lambda i: joint_block(twin, 16 + i), lc)
    right = right_operand(twin, lc, lambda r, u: tile(band, r, u), None, None)

    def keep(r, u, total):
        total = total + (tile(sums, r, u - 2) if u in OWN else tile(part_l, r, u))
        each_block(table, r, u, total, lambda row, t, b: put(sq, row, t, b.astype(BF)))

    def step(r, u, total):
        if u not in LEFT:
            total = total + tile(more, r, u - 2)

        def store(row, t, block):
            if u in RIGHT:
                now = sq_r[row * S : (row + 1) * S, (t - 8) * S : (t - 7) * S]
            else:
                now = sq[row * S : (row + 1) * S, t * S : (t + 1) * S]
            finish(row, t, (3.0 * now.astype(F32) - 2.0 * block).astype(BF))

        each_block(table, r, u, total, store)

    product(lambda r, t: left_tile(band, r, t) if t in LEFT else None, right, LEFT + OWN, keep)
    product(lambda r, t: None if t in RIGHT else left_tile(sq, r, t), right, columns, step)
    if after:
        after(0)
        after(1)


def step_kernel(table, band, sq_r, part_l, sums, more, twin, new, send, sq, lc):
    def finish(row, t, value):
        put(new, row, t, value)
        joint_send(send, row, t, value)

    late_kernel(OWN + RIGHT, table, band, sq_r, part_l, sums, more, twin, lc, sq, finish)


def step_left_kernel(table, band, sq, twin, new_in, new):
    new[H:, H:Q] = jnp.zeros((H, H), BF)
    new[:H, 2 * Q + H :] = jnp.zeros((H, H), BF)
    right = right_operand(twin, None, lambda r, u: tile(band, r, u), None, None)

    def step(r, u, total):
        def store(row, t, block):
            now = sq[row * S : (row + 1) * S, t * S : (t + 1) * S]
            put(new, row, t, (3.0 * now.astype(F32) - 2.0 * block).astype(BF))

        each_block(table, r, u, total, store)

    product(lambda r, t: None if t in RIGHT else left_tile(sq, r, t), right, LEFT, step)


def last_kernel(index, table, band, sq_r, part_l, sums, more, twin, out_hbm, *scratch):
    lc, sq, res, out, sems = scratch
    core = lax.axis_index("rep")

    def copy(row):
        return pltpu.make_async_copy(out.at[row], out_hbm.at[source_row(row)], sems.at[row])

    def after(half):
        for row in (2 * half, 2 * half + 1):
            for s in range(4):
                t = index[49 + 8 * row + core * 4 + s]
                block = res[row * S : (row + 1) * S, at(jnp.maximum(t, 0))]
                out[row, s] = jnp.where(t >= 0, block, jnp.zeros_like(block))
            copy(row).start()

    late_kernel(
        LEFT + OWN + RIGHT, table, band, sq_r, part_l, sums, more, twin, lc, sq,
        lambda row, t, value: put(res, row, t, value), after,
    )
    for row in range(4):
        copy(row).wait()


def join_kernel(band, side, out):
    out[:, Q:] = band[:, Q:]
    out[:H, 2 * Q + H :] = jnp.zeros((H, H), BF)
    spread_twin(lambda i: side[i], out.at[:, :Q])


def on_device(hamiltonian, x_correction, cols, mask):
    n = lax.axis_size("rows")
    factor = 0.6 / math.sqrt(cols.shape[1] * hamiltonian.shape[-1])
    outward = [(2 * i + 1, 2 * i + 2) for i in range(n - 1)] + [(2 * i, 2 * i - 1) for i in range(1, n)]

    def link(x):
        return lax.ppermute(x, ("rows", "rep"), outward)

    def swap(x):
        return lax.ppermute(x, "rep", [(0, 1), (1, 0)])

    square = pltpu.VMEM((Q, Q), BF)
    flops = 1 << 29
    hbm = pl.BlockSpec(memory_space=pltpu.HBM)

    index_table = pltpu.SMEM((81,), jnp.int32)
    h_send, table, h_rows = call(
        pack_h_kernel,
        [SEND, index_table, jax.ShapeDtypeStruct(hamiltonian.shape, BF)],
        [VMEM, SMEM, VMEM],
        [hbm] * 3,
        [
            pltpu.SMEM(cols.shape, jnp.int32),
            pltpu.SMEM(mask.shape, jnp.int32),
            pltpu.SemaphoreType.DMA((6,)),
        ],
        flops,
        *(pltpu.with_memory_space_constraint(x, pltpu.HBM) for x in (cols, mask, hamiltonian)),
    )
    h_halo = link(h_send)
    xa, xb, marks = call(
        pack_x_kernel,
        [CORNER, SQUARE, jax.ShapeDtypeStruct((48, S), F32)],
        [VMEM] * 3,
        [SMEM, VMEM],
        [],
        0,
        table, x_correction,
    )
    xa_halo = link(xa)
    xb_halo = link(xb)
    h_twin = swap(h_halo)
    xo, part = call(
        mine_kernel,
        [BANDED, WIDE],
        [VMEM] * 2,
        [SMEM] + [VMEM] * 3,
        [pltpu.VMEM((Q, 3 * Q), BF), square],
        64 * flops,
        table, h_rows, x_correction, h_halo,
    )
    xa_copy, x_corner = call(spread_kernel, [CORNER, SQUARE], [VMEM] * 2, [VMEM] * 2, [], 0, xa_halo, part)
    xa_twin = swap(xa_copy)
    half = call(half_kernel, BANDED, VMEM, [VMEM] + [VMEM] * 3, [square], 16 * flops, marks, xo, h_twin, part)
    band, send = call(
        lambda *refs: center_kernel(factor, *refs),
        [BANDED, SEND],
        [VMEM] * 2,
        [VMEM] * 5,
        [square],
        flops,
        marks, half, xo, x_corner, xa_twin,
    )
    band, send, side = call(
        lambda *refs: side_kernel(factor, *refs),
        [BANDED, SEND, CORNER],
        [VMEM] * 3,
        [VMEM] * 6,
        [],
        flops,
        marks, half, xo, xb_halo, band, send,
        alias={4: 0, 5: 1},
    )
    halo = link(send)
    band = call(join_kernel, BANDED, VMEM, [VMEM] * 2, [], 0, band, swap(side))
    for step in range(STEPS):
        if step > 0:
            halo = link(send)
        twin = swap(halo)
        sq_r, part_l, sums, more = call(
            mine_squares_kernel,
            [SQUARE, SUMS, SUMS, jax.ShapeDtypeStruct((Q, 2 * Q), F32)],
            [VMEM] * 4,
            [VMEM] + [VMEM] * 2,
            [square],
            64 * flops,
            marks, band, halo,
        )
        operands = (marks, band, sq_r, part_l, sums, more, twin)
        if step + 1 == STEPS:
            return call(
                last_kernel,
                jax.ShapeDtypeStruct((4, 4, S, S), BF),
                hbm,
                [SMEM] + [VMEM] * 7,
                [square, pltpu.VMEM((Q, 2 * Q), BF)]
                + [pltpu.VMEM((Q, 3 * Q), BF), pltpu.VMEM((4, 4, S, S), BF), pltpu.SemaphoreType.DMA((4,))],
                flops,
                table, *operands,
            )
        new, send, sq = call(
            step_kernel,
            [BANDED, SEND, jax.ShapeDtypeStruct((Q, 2 * Q), BF)],
            [VMEM] * 3,
            [VMEM] * 7,
            [square],
            flops,
            *operands,
        )
        band = call(
            step_left_kernel, BANDED, VMEM, [VMEM] * 5, [], 0, marks, band, sq, twin, new, alias={4: 0}
        )


def solution(mesh):
    return jax.shard_map(
        on_device,
        mesh=mesh,
        in_specs=(
            P("rows", None, None, None),
            P("rows", None, None, None),
            P("rows", None),
            P("rows", None),
        ),
        out_specs=P("rows", "rep", None, None),
        check_vma=False,
    )
```

```python
import math

import jax
import jax.numpy as jnp
from jax import lax
from jax.experimental import pallas as pl
from jax.experimental.pallas import tpu as pltpu
from jax.sharding import PartitionSpec as P

BAND = 4
STEPS = 2
S = 128
Q = 4 * S
H = 2 * S
TRI = [(p, m) for p in range(4) for m in range(p, 4)]
BF = jnp.bfloat16
F32 = jnp.float32
LEFT, OWN, RIGHT = (0, 1), (2, 3), (4, 5)

VMEM = pl.BlockSpec(memory_space=pltpu.VMEM)
SMEM = pl.BlockSpec(memory_space=pltpu.SMEM)
SQUARE = jax.ShapeDtypeStruct((Q, Q), BF)
CORNER = jax.ShapeDtypeStruct((len(TRI), S, S), BF)
BANDED = jax.ShapeDtypeStruct((Q, 3 * Q), BF)
SEND = jax.ShapeDtypeStruct((6 * S + S // 2, Q), BF)
SUMS = jax.ShapeDtypeStruct((Q, Q), F32)
WIDE = jax.ShapeDtypeStruct((Q, 3 * Q), F32)


def call(kernel, outs, out_specs, in_specs, scratch, flops, *args, room=24, alias=None):
    return pl.pallas_call(
        kernel,
        out_shape=outs,
        in_specs=in_specs,
        out_specs=out_specs,
        scratch_shapes=scratch,
        input_output_aliases=alias or {},
        compiler_params=pltpu.CompilerParams(vmem_limit_bytes=room << 20),
        cost_estimate=pl.CostEstimate(flops=flops, bytes_accessed=4 << 20, transcendentals=0),
    )(*args)


def place(cols_ref, mask_ref, a, s):
    first = lax.axis_index("rows") * 4 - BAND
    core = lax.axis_index("rep")
    k = cols_ref[a, s] - first
    k = jnp.clip(k, 0, 11)
    k = jnp.where(core == 0, 11 - k, k)
    row = jnp.where(core == 0, 3 - a, a)
    t = jnp.where(k < 4, 3 - k, k)
    return mask_ref[a, s] == 1, row, t


def at(index):
    return pl.ds(pl.multiple_of(index * S, S), S)


def eye():
    rows = lax.broadcasted_iota(jnp.int32, (S, S), 0)
    cols = lax.broadcasted_iota(jnp.int32, (S, S), 1)
    return (rows == cols).astype(F32)


def joint_put(joint, index, block):
    if index >= 24:
        col = (index - 24) * 2 * S
        joint[6 * S :, col : col + S] = block[: S // 2]
        joint[6 * S :, col + S : col + 2 * S] = block[S // 2 :]
    else:
        row, col = index // 4 * S, index % 4 * S
        joint[row : row + S, col : col + S] = block


def joint_block(joint, index):
    if index >= 24:
        col = (index - 24) * 2 * S
        return jnp.concatenate([joint[6 * S :, col : col + S], joint[6 * S :, col + S : col + 2 * S]], axis=0)
    row, col = index // 4 * S, index % 4 * S
    return joint[row : row + S, col : col + S]


def joint_send(joint, row, t, block):
    if 4 <= t < 8:
        joint_put(joint, 4 * (3 - row) + 7 - t, block)
    if t >= 8 and (3 - row, 11 - t) in TRI:
        joint_put(joint, 16 + TRI.index((3 - row, 11 - t)), block)


def fill_table(cols, mask, table):
    for i in range(48):
        table[i] = -1
    for a in range(4):
        for s in range(8):
            active, row, t = place(cols, mask, a, s)
            table[jnp.where(active, 12 * row + t, 48)] = s
            table[49 + 8 * row + s] = jnp.where(active, t, -1)


def source_row(row):
    return jnp.where(lax.axis_index("rep") == 0, 3 - row, row)


def row_block(ref, table, row, t, source=None):
    slot = table[12 * row + t]
    block = ref[row if source is None else source, jnp.maximum(slot, 0)]
    return jnp.where(slot >= 0, block, jnp.zeros_like(block))


def slot_block(ref, table, row, t):
    return row_block(ref, table, row, t, source_row(row))


def x_slot_block(ref, table, diag, row, t):
    block = slot_block(ref, table, row, t)
    return (block.astype(F32) + diag).astype(BF) if t - 4 == row else block


def pack_h_kernel(cols_hbm, mask_hbm, h_hbm, send, table, h_ref, cols, mask, sems):
    pattern = [
        pltpu.make_async_copy(cols_hbm, cols, sems.at[0]),
        pltpu.make_async_copy(mask_hbm, mask, sems.at[1]),
    ]
    rows = [pltpu.make_async_copy(h_hbm.at[source_row(row)], h_ref.at[row], sems.at[2 + row]) for row in range(4)]
    for copy in pattern + rows:
        copy.start()
    for copy in pattern:
        copy.wait()
    fill_table(cols, mask, table)
    for row in range(4):
        rows[row].wait()
        for t in range(4, 12):
            joint_send(send, row, t, row_block(h_ref, table, row, t))


def pack_x_kernel(table, x_ref, xa, xb, marks):
    diag = eye()
    for index, (p, m) in enumerate(TRI):
        xa[index] = slot_block(x_ref, table, 3 - p, 11 - m)
    for row in range(4):
        for m in range(4):
            put(xb, 3 - row, 3 - m, x_slot_block(x_ref, table, diag, row, 4 + m))
    for i in range(48):
        marks[i : i + 1, :] = jnp.full((1, S), jnp.where(table[i] >= 0, 1.0, 0.0), F32)


def spread_mine(get, square_ref):
    square_ref[H:, :H] = jnp.zeros((H, H), BF)
    square_ref[S : 2 * S, :S] = jnp.zeros((S, S), BF)
    square_ref[3 * S :, H : 3 * S] = jnp.zeros((S, S), BF)
    for index, (p, m) in enumerate(TRI):
        square_ref[p * S : (p + 1) * S, m * S : (m + 1) * S] = get(index)


def spread_twin(get, square_ref):
    square_ref[H:, H:] = jnp.zeros((H, H), BF)
    square_ref[S : 2 * S, 3 * S :] = jnp.zeros((S, S), BF)
    square_ref[3 * S :, S:H] = jnp.zeros((S, S), BF)
    for index, (p, m) in enumerate(TRI):
        square_ref[p * S : (p + 1) * S, (3 - m) * S : (4 - m) * S] = get(index)


def tile(ref, i, j):
    return ref[i * H : (i + 1) * H, j * H : (j + 1) * H]


def right_operand(ll, lc, own, rc, rr):
    def get(t, u):
        if t in OWN:
            if (t, u) in ((3, 1), (2, 5)):
                return None
            return own(t - 2, u)
        if t in LEFT:
            if u in LEFT:
                return tile(ll, t, u)
            if u in OWN and (t, u) != (1, 3):
                return tile(lc, t, u - 2)
            return None
        if u in RIGHT:
            return tile(rr, t - 4, u - 4)
        if u in OWN and (t, u) != (5, 2):
            return tile(rc, t - 4, u - 2)
        return None

    return get


def left_tile(ref, r, t):
    if (r, t) in ((1, 1), (0, 5)):
        return None
    return tile(ref, r, t)


def product(left, right, columns, finish, rows=(0, 1)):
    for u in columns:
        for r in rows:
            if (r, u) in ((1, 1), (0, 5)):
                continue
            xs, ys = [], []
            for t in range(6):
                x = left(r, t)
                y = None if x is None else right(t, u)
                if y is not None:
                    xs.append(x)
                    ys.append(y)
            total = None
            if xs:
                x, y = jnp.concatenate(xs, axis=1), jnp.concatenate(ys, axis=0)
                total = jnp.dot(x, y, preferred_element_type=F32)
            finish(r, u, total)


def each_block(table_ref, r, u, total, store):
    for i in range(2):
        for j in range(2):
            row, t = 2 * r + i, 2 * u + j
            block = total[i * S : (i + 1) * S, j * S : (j + 1) * S]
            block = jnp.where(table_ref[12 * row + t : 12 * row + t + 1, :] > 0.0, block, 0.0)
            store(row, t, block)


def put(ref, row, t, block):
    ref[row * S : (row + 1) * S, t * S : (t + 1) * S] = block


def put_tile(ref, i, j, value):
    ref[i * H : (i + 1) * H, j * H : (j + 1) * H] = value


def mine_kernel(table, h_ref, x_ref, joint, xo, part, ho, rc):
    diag = eye()
    for row in range(4):
        for t in range(12):
            put(ho, row, t, row_block(h_ref, table, row, t))
            put(xo, row, t, x_slot_block(x_ref, table, diag, row, t))
    spread_mine(lambda i: joint_block(joint, 16 + i), rc)
    right = right_operand(None, None, lambda r, u: tile(ho, r, u), rc, joint)
    left = lambda r, t: None if t in LEFT else left_tile(xo, r, t)
    product(left, right, range(6), lambda r, u, total: put_tile(part, r, u, total))


def spread_kernel(xa, part, copy, square):
    copy[...] = xa[...]
    spread_mine(lambda i: xa[i], square)


def half_kernel(table, xo, twin, part, half_ref, lc):
    spread_twin(lambda i: joint_block(twin, 16 + i), lc)
    half_ref[H:, H:Q] = jnp.zeros((H, H), BF)
    half_ref[:H, 2 * Q + H :] = jnp.zeros((H, H), BF)
    right = right_operand(twin, lc, None, None, None)

    def keep(r, u, total):
        total = tile(part, r, u) if total is None else total + tile(part, r, u)
        each_block(table, r, u, total, lambda row, t, b: put(half_ref, row, t, b.astype(BF)))

    product(lambda r, t: left_tile(xo, r, t) if t in LEFT else None, right, range(6), keep)


def center_kernel(factor, table, half, xo, xrc, xa2, band, send, begun, xlc):
    spread_twin(lambda i: xa2[i], xlc)
    right = right_operand(None, xlc, lambda r, u: tile(xo, r, u), xrc, None)
    diag = eye()

    def start(r, u, total):
        def store(row, t, block):
            value = -factor * block
            if t - 4 == row:
                value = value + 0.5 * diag
            value = value.astype(BF)
            put(band, row, t, value)
            joint_send(send, row, t, value)

        each_block(table, r, u, total, store)

    product(lambda r, t: left_tile(half, r, t), right, OWN, start)
    product(
        lambda r, t: left_tile(half, r, t) if t in OWN else None,
        right,
        RIGHT,
        lambda r, u, total: put_tile(begun, r, u - 4, total),
    )


def side_kernel(factor, table, half, begun, xb, band_in, send_in, band, send, side):
    right = right_operand(None, None, None, None, xb)

    def start(r, u, total):
        total = total + tile(begun, r, u - 4)

        def store(row, t, block):
            value = (-factor * block).astype(BF)
            put(band, row, t, value)
            joint_send(send, row, t, value)
            if (3 - row, 11 - t) in TRI:
                side[TRI.index((3 - row, 11 - t))] = value

        each_block(table, r, u, total, store)

    product(lambda r, t: left_tile(half, r, t) if t in RIGHT else None, right, RIGHT, start)


def mine_squares_kernel(table, band, joint, sq_r, part_l, sums, more, rc):
    spread_mine(lambda i: joint_block(joint, 16 + i), rc)
    sq_r[:H, H:] = jnp.zeros((H, H), BF)
    right = right_operand(None, None, lambda r, u: tile(band, r, u), rc, joint)

    def keep(r, u, total):
        if u in LEFT:
            put_tile(part_l, r, u, total)
        elif u in OWN:
            put_tile(sums, r, u - 2, total)
        else:
            each_block(table, r, u, total, lambda row, t, b: put(sq_r, row, t - 8, b.astype(BF)))

    product(lambda r, t: None if t in LEFT else left_tile(band, r, t), right, RIGHT + OWN + LEFT, keep)

    def square(r, t):
        return None if t not in RIGHT or (r, t) == (0, 5) else tile(sq_r, r, t - 4)

    product(square, right, OWN + RIGHT, lambda r, u, total: put_tile(more, r, u - 2, total))


def late_kernel(columns, table, band, sq_r, part_l, sums, more, twin, lc, sq, finish, after=None):
    spread_twin(lambda i: joint_block(twin, 16 + i), lc)
    right = right_operand(twin, lc, lambda r, u: tile(band, r, u), None, None)

    def keep(r, u, total):
        total = total + (tile(sums, r, u - 2) if u in OWN else tile(part_l, r, u))
        each_block(table, r, u, total, lambda row, t, b: put(sq, row, t, b.astype(BF)))

    def step(r, u, total):
        if u not in LEFT:
            total = total + tile(more, r, u - 2)

        def store(row, t, block):
            if u in RIGHT:
                now = sq_r[row * S : (row + 1) * S, (t - 8) * S : (t - 7) * S]
            else:
                now = sq[row * S : (row + 1) * S, t * S : (t + 1) * S]
            finish(row, t, (3.0 * now.astype(F32) - 2.0 * block).astype(BF))

        each_block(table, r, u, total, store)

    product(lambda r, t: left_tile(band, r, t) if t in LEFT else None, right, LEFT + OWN, keep)
    for half in range(2):
        product(lambda r, t: None if t in RIGHT else left_tile(sq, r, t), right, columns, step, (half,))
        if after:
            after(half)


def step_kernel(table, band, sq_r, part_l, sums, more, twin, new, send, sq, lc):
    def finish(row, t, value):
        put(new, row, t, value)
        joint_send(send, row, t, value)

    late_kernel(OWN + RIGHT, table, band, sq_r, part_l, sums, more, twin, lc, sq, finish)


def step_left_kernel(table, band, sq, twin, new_in, new):
    new[H:, H:Q] = jnp.zeros((H, H), BF)
    new[:H, 2 * Q + H :] = jnp.zeros((H, H), BF)
    right = right_operand(twin, None, lambda r, u: tile(band, r, u), None, None)

    def step(r, u, total):
        def store(row, t, block):
            now = sq[row * S : (row + 1) * S, t * S : (t + 1) * S]
            put(new, row, t, (3.0 * now.astype(F32) - 2.0 * block).astype(BF))

        each_block(table, r, u, total, store)

    product(lambda r, t: None if t in RIGHT else left_tile(sq, r, t), right, LEFT, step)


def last_kernel(index, table, band, sq_r, part_l, sums, more, twin, out_hbm, *scratch):
    lc, sq, res, out, sems = scratch
    core = lax.axis_index("rep")

    def copy(row):
        return pltpu.make_async_copy(out.at[row], out_hbm.at[source_row(row)], sems.at[row])

    def after(half):
        for row in (2 * half, 2 * half + 1):
            for s in range(4):
                t = index[49 + 8 * row + core * 4 + s]
                block = res[row * S : (row + 1) * S, at(jnp.maximum(t, 0))]
                out[row, s] = jnp.where(t >= 0, block, jnp.zeros_like(block))
            copy(row).start()

    late_kernel(
        LEFT + OWN + RIGHT, table, band, sq_r, part_l, sums, more, twin, lc, sq,
        lambda row, t, value: put(res, row, t, value), after,
    )
    for row in range(4):
        copy(row).wait()


def join_kernel(band, side, out):
    out[:, Q:] = band[:, Q:]
    out[:H, 2 * Q + H :] = jnp.zeros((H, H), BF)
    spread_twin(lambda i: side[i], out.at[:, :Q])


def on_device(hamiltonian, x_correction, cols, mask):
    n = lax.axis_size("rows")
    factor = 0.6 / math.sqrt(cols.shape[1] * hamiltonian.shape[-1])
    outward = [(2 * i + 1, 2 * i + 2) for i in range(n - 1)] + [(2 * i, 2 * i - 1) for i in range(1, n)]

    def link(x):
        return lax.ppermute(x, ("rows", "rep"), outward)

    def swap(x):
        return lax.ppermute(x, "rep", [(0, 1), (1, 0)])

    square = pltpu.VMEM((Q, Q), BF)
    flops = 1 << 29
    hbm = pl.BlockSpec(memory_space=pltpu.HBM)

    index_table = pltpu.SMEM((81,), jnp.int32)
    h_send, table, h_rows = call(
        pack_h_kernel,
        [SEND, index_table, jax.ShapeDtypeStruct(hamiltonian.shape, BF)],
        [VMEM, SMEM, VMEM],
        [hbm] * 3,
        [
            pltpu.SMEM(cols.shape, jnp.int32),
            pltpu.SMEM(mask.shape, jnp.int32),
            pltpu.SemaphoreType.DMA((6,)),
        ],
        flops,
        *(pltpu.with_memory_space_constraint(x, pltpu.HBM) for x in (cols, mask, hamiltonian)),
    )
    h_halo = link(h_send)
    xa, xb, marks = call(
        pack_x_kernel,
        [CORNER, SQUARE, jax.ShapeDtypeStruct((48, S), F32)],
        [VMEM] * 3,
        [SMEM, VMEM],
        [],
        0,
        table, x_correction,
    )
    xa_halo = link(xa)
    xb_halo = link(xb)
    h_twin = swap(h_halo)
    xo, part = call(
        mine_kernel,
        [BANDED, WIDE],
        [VMEM] * 2,
        [SMEM] + [VMEM] * 3,
        [pltpu.VMEM((Q, 3 * Q), BF), square],
        64 * flops,
        table, h_rows, x_correction, h_halo,
    )
    xa_copy, x_corner = call(spread_kernel, [CORNER, SQUARE], [VMEM] * 2, [VMEM] * 2, [], 0, xa_halo, part)
    xa_twin = swap(xa_copy)
    half = call(half_kernel, BANDED, VMEM, [VMEM] + [VMEM] * 3, [square], 16 * flops, marks, xo, h_twin, part)
    band, send, begun = call(
        lambda *refs: center_kernel(factor, *refs),
        [BANDED, SEND, SUMS],
        [VMEM] * 3,
        [VMEM] * 5,
        [square],
        flops,
        marks, half, xo, x_corner, xa_twin,
    )
    band, send, side = call(
        lambda *refs: side_kernel(factor, *refs),
        [BANDED, SEND, CORNER],
        [VMEM] * 3,
        [VMEM] * 6,
        [],
        flops,
        marks, half, begun, xb_halo, band, send,
        alias={4: 0, 5: 1},
    )
    halo = link(send)
    band = call(join_kernel, BANDED, VMEM, [VMEM] * 2, [], 0, band, swap(side))
    for step in range(STEPS):
        if step > 0:
            halo = link(send)
        twin = swap(halo)
        sq_r, part_l, sums, more = call(
            mine_squares_kernel,
            [SQUARE, SUMS, SUMS, jax.ShapeDtypeStruct((Q, 2 * Q), F32)],
            [VMEM] * 4,
            [VMEM] + [VMEM] * 2,
            [square],
            64 * flops,
            marks, band, halo,
        )
        operands = (marks, band, sq_r, part_l, sums, more, twin)
        if step + 1 == STEPS:
            return call(
                last_kernel,
                jax.ShapeDtypeStruct((4, 4, S, S), BF),
                hbm,
                [SMEM] + [VMEM] * 7,
                [square, pltpu.VMEM((Q, 2 * Q), BF)]
                + [pltpu.VMEM((Q, 3 * Q), BF), pltpu.VMEM((4, 4, S, S), BF), pltpu.SemaphoreType.DMA((4,))],
                flops,
                table, *operands,
            )
        new, send, sq = call(
            step_kernel,
            [BANDED, SEND, jax.ShapeDtypeStruct((Q, 2 * Q), BF)],
            [VMEM] * 3,
            [VMEM] * 7,
            [square],
            flops,
            *operands,
        )
        band = call(
            step_left_kernel, BANDED, VMEM, [VMEM] * 5, [], 0, marks, band, sq, twin, new, alias={4: 0}
        )


def solution(mesh):
    return jax.shard_map(
        on_device,
        mesh=mesh,
        in_specs=(
            P("rows", None, None, None),
            P("rows", None, None, None),
            P("rows", None),
            P("rows", None),
        ),
        out_specs=P("rows", "rep", None, None),
        check_vma=False,
    )
```

```python
import math

import jax
import jax.numpy as jnp
from jax import lax
from jax.experimental import pallas as pl
from jax.experimental.pallas import tpu as pltpu
from jax.sharding import PartitionSpec as P

BAND = 4
STEPS = 2
S = 128
Q = 4 * S
H = 2 * S
TRI = [(p, m) for p in range(4) for m in range(p, 4)]
BF = jnp.bfloat16
F32 = jnp.float32
LEFT, OWN, RIGHT = (0, 1), (2, 3), (4, 5)

VMEM = pl.BlockSpec(memory_space=pltpu.VMEM)
SMEM = pl.BlockSpec(memory_space=pltpu.SMEM)
SQUARE = jax.ShapeDtypeStruct((Q, Q), BF)
CORNER = jax.ShapeDtypeStruct((len(TRI), S, S), BF)
BANDED = jax.ShapeDtypeStruct((Q, 3 * Q), BF)
SEND = jax.ShapeDtypeStruct((6 * S + S // 2, Q), BF)
SUMS = jax.ShapeDtypeStruct((Q, Q), F32)
WIDE = jax.ShapeDtypeStruct((Q, 3 * Q), F32)


def call(kernel, outs, out_specs, in_specs, scratch, flops, *args, room=24, alias=None):
    return pl.pallas_call(
        kernel,
        out_shape=outs,
        in_specs=in_specs,
        out_specs=out_specs,
        scratch_shapes=scratch,
        input_output_aliases=alias or {},
        compiler_params=pltpu.CompilerParams(vmem_limit_bytes=room << 20),
        cost_estimate=pl.CostEstimate(flops=flops, bytes_accessed=4 << 20, transcendentals=0),
    )(*args)


def place(cols_ref, mask_ref, a, s):
    first = lax.axis_index("rows") * 4 - BAND
    core = lax.axis_index("rep")
    k = cols_ref[a, s] - first
    k = jnp.clip(k, 0, 11)
    k = jnp.where(core == 0, 11 - k, k)
    row = jnp.where(core == 0, 3 - a, a)
    t = jnp.where(k < 4, 3 - k, k)
    return mask_ref[a, s] == 1, row, t


def at(index):
    return pl.ds(pl.multiple_of(index * S, S), S)


def eye():
    rows = lax.broadcasted_iota(jnp.int32, (S, S), 0)
    cols = lax.broadcasted_iota(jnp.int32, (S, S), 1)
    return (rows == cols).astype(F32)


def joint_put(joint, index, block):
    if index >= 24:
        col = (index - 24) * 2 * S
        joint[6 * S :, col : col + S] = block[: S // 2]
        joint[6 * S :, col + S : col + 2 * S] = block[S // 2 :]
    else:
        row, col = index // 4 * S, index % 4 * S
        joint[row : row + S, col : col + S] = block


def joint_block(joint, index):
    if index >= 24:
        col = (index - 24) * 2 * S
        return jnp.concatenate([joint[6 * S :, col : col + S], joint[6 * S :, col + S : col + 2 * S]], axis=0)
    row, col = index // 4 * S, index % 4 * S
    return joint[row : row + S, col : col + S]


def joint_send(joint, row, t, block):
    if 4 <= t < 8:
        joint_put(joint, 4 * (3 - row) + 7 - t, block)
    if t >= 8 and (3 - row, 11 - t) in TRI:
        joint_put(joint, 16 + TRI.index((3 - row, 11 - t)), block)


def fill_table(cols, mask, table):
    for i in range(48):
        table[i] = -1
    for a in range(4):
        for s in range(8):
            active, row, t = place(cols, mask, a, s)
            table[jnp.where(active, 12 * row + t, 48)] = s
            table[49 + 8 * row + s] = jnp.where(active, t, -1)


def source_row(row):
    return jnp.where(lax.axis_index("rep") == 0, 3 - row, row)


def row_block(ref, table, row, t, source=None):
    slot = table[12 * row + t]
    block = ref[row if source is None else source, jnp.maximum(slot, 0)]
    return jnp.where(slot >= 0, block, jnp.zeros_like(block))


def slot_block(ref, table, row, t):
    return row_block(ref, table, row, t, source_row(row))


def x_slot_block(ref, table, diag, row, t):
    block = slot_block(ref, table, row, t)
    return (block.astype(F32) + diag).astype(BF) if t - 4 == row else block


def pack_h_kernel(cols_hbm, mask_hbm, h_hbm, send, table, h_ref, cols, mask, sems):
    pattern = [
        pltpu.make_async_copy(cols_hbm, cols, sems.at[0]),
        pltpu.make_async_copy(mask_hbm, mask, sems.at[1]),
    ]
    rows = [pltpu.make_async_copy(h_hbm.at[source_row(row)], h_ref.at[row], sems.at[2 + row]) for row in range(4)]
    for copy in pattern + rows:
        copy.start()
    for copy in pattern:
        copy.wait()
    fill_table(cols, mask, table)
    for row in range(4):
        rows[row].wait()
        for t in range(4, 12):
            joint_send(send, row, t, row_block(h_ref, table, row, t))


def pack_x_kernel(table, x_ref, xa, xb):
    diag = eye()
    for index, (p, m) in enumerate(TRI):
        xa[index] = slot_block(x_ref, table, 3 - p, 11 - m)
    for row in range(4):
        for m in range(4):
            put(xb, 3 - row, 3 - m, x_slot_block(x_ref, table, diag, row, 4 + m))


def spread_mine(get, square_ref):
    square_ref[H:, :H] = jnp.zeros((H, H), BF)
    square_ref[S : 2 * S, :S] = jnp.zeros((S, S), BF)
    square_ref[3 * S :, H : 3 * S] = jnp.zeros((S, S), BF)
    for index, (p, m) in enumerate(TRI):
        square_ref[p * S : (p + 1) * S, m * S : (m + 1) * S] = get(index)


def spread_twin(get, square_ref):
    square_ref[H:, H:] = jnp.zeros((H, H), BF)
    square_ref[S : 2 * S, 3 * S :] = jnp.zeros((S, S), BF)
    square_ref[3 * S :, S:H] = jnp.zeros((S, S), BF)
    for index, (p, m) in enumerate(TRI):
        square_ref[p * S : (p + 1) * S, (3 - m) * S : (4 - m) * S] = get(index)


def tile(ref, i, j):
    return ref[i * H : (i + 1) * H, j * H : (j + 1) * H]


def right_operand(ll, lc, own, rc, rr):
    def get(t, u):
        if t in OWN:
            if (t, u) in ((3, 1), (2, 5)):
                return None
            return own(t - 2, u)
        if t in LEFT:
            if u in LEFT:
                return tile(ll, t, u)
            if u in OWN and (t, u) != (1, 3):
                return tile(lc, t, u - 2)
            return None
        if u in RIGHT:
            return tile(rr, t - 4, u - 4)
        if u in OWN and (t, u) != (5, 2):
            return tile(rc, t - 4, u - 2)
        return None

    return get


def left_tile(ref, r, t):
    if (r, t) in ((1, 1), (0, 5)):
        return None
    return tile(ref, r, t)


def product(left, right, columns, finish):
    for u in columns:
        for r in range(2):
            if (r, u) in ((1, 1), (0, 5)):
                continue
            xs, ys = [], []
            for t in range(6):
                x = left(r, t)
                y = None if x is None else right(t, u)
                if y is not None:
                    xs.append(x)
                    ys.append(y)
            total = None
            if xs:
                x, y = jnp.concatenate(xs, axis=1), jnp.concatenate(ys, axis=0)
                total = jnp.dot(x, y, preferred_element_type=F32)
            finish(r, u, total)


def each_block(table_ref, r, u, total, store):
    for i in range(2):
        for j in range(2):
            row, t = 2 * r + i, 2 * u + j
            block = total[i * S : (i + 1) * S, j * S : (j + 1) * S]
            block = jnp.where(table_ref[12 * row + t : 12 * row + t + 1, :] > 0.0, block, 0.0)
            store(row, t, block)


def put(ref, row, t, block):
    ref[row * S : (row + 1) * S, t * S : (t + 1) * S] = block


def put_tile(ref, i, j, value):
    ref[i * H : (i + 1) * H, j * H : (j + 1) * H] = value


def mine_kernel(table, h_ref, x_ref, joint, xo, part, marks, ho, rc):
    for i in range(48):
        marks[i : i + 1, :] = jnp.full((1, S), jnp.where(table[i] >= 0, 1.0, 0.0), F32)
    diag = eye()
    for row in range(4):
        for t in range(12):
            put(ho, row, t, row_block(h_ref, table, row, t))
            put(xo, row, t, x_slot_block(x_ref, table, diag, row, t))
    spread_mine(lambda i: joint_block(joint, 16 + i), rc)
    right = right_operand(None, None, lambda r, u: tile(ho, r, u), rc, joint)
    left = lambda r, t: None if t in LEFT else left_tile(xo, r, t)
    product(left, right, range(6), lambda r, u, total: put_tile(part, r, u, total))


def spread_kernel(xa, part, copy, square):
    copy[...] = xa[...]
    spread_mine(lambda i: xa[i], square)


def half_kernel(table, xo, twin, part, half_ref, lc):
    spread_twin(lambda i: joint_block(twin, 16 + i), lc)
    half_ref[H:, H:Q] = jnp.zeros((H, H), BF)
    half_ref[:H, 2 * Q + H :] = jnp.zeros((H, H), BF)
    right = right_operand(twin, lc, None, None, None)

    def keep(r, u, total):
        total = tile(part, r, u) if total is None else total + tile(part, r, u)
        each_block(table, r, u, total, lambda row, t, b: put(half_ref, row, t, b.astype(BF)))

    product(lambda r, t: left_tile(xo, r, t) if t in LEFT else None, right, range(6), keep)


def center_kernel(factor, table, half, xo, xrc, xa2, band, send, xlc):
    spread_twin(lambda i: xa2[i], xlc)
    right = right_operand(None, xlc, lambda r, u: tile(xo, r, u), xrc, None)
    diag = eye()

    def start(r, u, total):
        def store(row, t, block):
            value = -factor * block
            if t - 4 == row:
                value = value + 0.5 * diag
            value = value.astype(BF)
            put(band, row, t, value)
            joint_send(send, row, t, value)

        each_block(table, r, u, total, store)

    product(lambda r, t: left_tile(half, r, t), right, OWN, start)


def side_kernel(factor, table, half, xo, xb, band_in, send_in, band, send, side):
    right = right_operand(None, None, lambda r, u: tile(xo, r, u), None, xb)

    def start(r, u, total):
        def store(row, t, block):
            value = (-factor * block).astype(BF)
            put(band, row, t, value)
            joint_send(send, row, t, value)
            if (3 - row, 11 - t) in TRI:
                side[TRI.index((3 - row, 11 - t))] = value

        each_block(table, r, u, total, store)

    product(lambda r, t: left_tile(half, r, t), right, RIGHT, start)


def mine_squares_kernel(table, band, joint, sq_r, part_l, sums, more, rc):
    spread_mine(lambda i: joint_block(joint, 16 + i), rc)
    sq_r[:H, H:] = jnp.zeros((H, H), BF)
    right = right_operand(None, None, lambda r, u: tile(band, r, u), rc, joint)

    def keep(r, u, total):
        if u in LEFT:
            put_tile(part_l, r, u, total)
        elif u in OWN:
            put_tile(sums, r, u - 2, total)
        else:
            each_block(table, r, u, total, lambda row, t, b: put(sq_r, row, t - 8, b.astype(BF)))

    product(lambda r, t: None if t in LEFT else left_tile(band, r, t), right, RIGHT + OWN + LEFT, keep)

    def square(r, t):
        return None if t not in RIGHT or (r, t) == (0, 5) else tile(sq_r, r, t - 4)

    product(square, right, OWN + RIGHT, lambda r, u, total: put_tile(more, r, u - 2, total))


def late_kernel(columns, table, band, sq_r, part_l, sums, more, twin, lc, sq, finish, after=None):
    spread_twin(lambda i: joint_block(twin, 16 + i), lc)
    right = right_operand(twin, lc, lambda r, u: tile(band, r, u), None, None)

    def keep(r, u, total):
        total = total + (tile(sums, r, u - 2) if u in OWN else tile(part_l, r, u))
        each_block(table, r, u, total, lambda row, t, b: put(sq, row, t, b.astype(BF)))

    def step(r, u, total):
        if u not in LEFT:
            total = total + tile(more, r, u - 2)

        def store(row, t, block):
            if u in RIGHT:
                now = sq_r[row * S : (row + 1) * S, (t - 8) * S : (t - 7) * S]
            else:
                now = sq[row * S : (row + 1) * S, t * S : (t + 1) * S]
            finish(row, t, (3.0 * now.astype(F32) - 2.0 * block).astype(BF))

        each_block(table, r, u, total, store)

    product(lambda r, t: left_tile(band, r, t) if t in LEFT else None, right, LEFT + OWN, keep)
    product(lambda r, t: None if t in RIGHT else left_tile(sq, r, t), right, columns, step)
    if after:
        after(0)
        after(1)


def step_kernel(table, band, sq_r, part_l, sums, more, twin, new, send, sq, lc):
    def finish(row, t, value):
        put(new, row, t, value)
        joint_send(send, row, t, value)

    late_kernel(OWN + RIGHT, table, band, sq_r, part_l, sums, more, twin, lc, sq, finish)


def step_left_kernel(table, band, sq, twin, new_in, new):
    new[H:, H:Q] = jnp.zeros((H, H), BF)
    new[:H, 2 * Q + H :] = jnp.zeros((H, H), BF)
    right = right_operand(twin, None, lambda r, u: tile(band, r, u), None, None)

    def step(r, u, total):
        def store(row, t, block):
            now = sq[row * S : (row + 1) * S, t * S : (t + 1) * S]
            put(new, row, t, (3.0 * now.astype(F32) - 2.0 * block).astype(BF))

        each_block(table, r, u, total, store)

    product(lambda r, t: None if t in RIGHT else left_tile(sq, r, t), right, LEFT, step)


def last_kernel(index, table, band, sq_r, part_l, sums, more, twin, out_hbm, *scratch):
    lc, sq, res, out, sems = scratch
    core = lax.axis_index("rep")

    def copy(row):
        return pltpu.make_async_copy(out.at[row], out_hbm.at[source_row(row)], sems.at[row])

    def after(half):
        for row in (2 * half, 2 * half + 1):
            for s in range(4):
                t = index[49 + 8 * row + core * 4 + s]
                block = res[row * S : (row + 1) * S, at(jnp.maximum(t, 0))]
                out[row, s] = jnp.where(t >= 0, block, jnp.zeros_like(block))
            copy(row).start()

    late_kernel(
        LEFT + OWN + RIGHT, table, band, sq_r, part_l, sums, more, twin, lc, sq,
        lambda row, t, value: put(res, row, t, value), after,
    )
    for row in range(4):
        copy(row).wait()


def join_kernel(band, side, out):
    out[:, Q:] = band[:, Q:]
    out[:H, 2 * Q + H :] = jnp.zeros((H, H), BF)
    spread_twin(lambda i: side[i], out.at[:, :Q])


def on_device(hamiltonian, x_correction, cols, mask):
    n = lax.axis_size("rows")
    factor = 0.6 / math.sqrt(cols.shape[1] * hamiltonian.shape[-1])
    outward = [(2 * i + 1, 2 * i + 2) for i in range(n - 1)] + [(2 * i, 2 * i - 1) for i in range(1, n)]

    def link(x):
        return lax.ppermute(x, ("rows", "rep"), outward)

    def swap(x):
        return lax.ppermute(x, "rep", [(0, 1), (1, 0)])

    square = pltpu.VMEM((Q, Q), BF)
    flops = 1 << 29
    hbm = pl.BlockSpec(memory_space=pltpu.HBM)

    index_table = pltpu.SMEM((81,), jnp.int32)
    h_send, table, h_rows = call(
        pack_h_kernel,
        [SEND, index_table, jax.ShapeDtypeStruct(hamiltonian.shape, BF)],
        [VMEM, SMEM, VMEM],
        [hbm] * 3,
        [
            pltpu.SMEM(cols.shape, jnp.int32),
            pltpu.SMEM(mask.shape, jnp.int32),
            pltpu.SemaphoreType.DMA((6,)),
        ],
        flops,
        *(pltpu.with_memory_space_constraint(x, pltpu.HBM) for x in (cols, mask, hamiltonian)),
    )
    h_halo = link(h_send)
    xa, xb = call(
        pack_x_kernel,
        [CORNER, SQUARE],
        [VMEM] * 2,
        [SMEM, VMEM],
        [],
        0,
        table, x_correction,
    )
    xa_halo = link(xa)
    xb_halo = link(xb)
    h_twin = swap(h_halo)
    xo, part, marks = call(
        mine_kernel,
        [BANDED, WIDE, jax.ShapeDtypeStruct((48, S), F32)],
        [VMEM] * 3,
        [SMEM] + [VMEM] * 3,
        [pltpu.VMEM((Q, 3 * Q), BF), square],
        64 * flops,
        table, h_rows, x_correction, h_halo,
    )
    xa_copy, x_corner = call(spread_kernel, [CORNER, SQUARE], [VMEM] * 2, [VMEM] * 2, [], 0, xa_halo, part)
    xa_twin = swap(xa_copy)
    half = call(half_kernel, BANDED, VMEM, [VMEM] + [VMEM] * 3, [square], 16 * flops, marks, xo, h_twin, part)
    band, send = call(
        lambda *refs: center_kernel(factor, *refs),
        [BANDED, SEND],
        [VMEM] * 2,
        [VMEM] * 5,
        [square],
        flops,
        marks, half, xo, x_corner, xa_twin,
    )
    band, send, side = call(
        lambda *refs: side_kernel(factor, *refs),
        [BANDED, SEND, CORNER],
        [VMEM] * 3,
        [VMEM] * 6,
        [],
        flops,
        marks, half, xo, xb_halo, band, send,
        alias={4: 0, 5: 1},
    )
    halo = link(send)
    band = call(join_kernel, BANDED, VMEM, [VMEM] * 2, [], 0, band, swap(side))
    for step in range(STEPS):
        if step > 0:
            halo = link(send)
        twin = swap(halo)
        sq_r, part_l, sums, more = call(
            mine_squares_kernel,
            [SQUARE, SUMS, SUMS, jax.ShapeDtypeStruct((Q, 2 * Q), F32)],
            [VMEM] * 4,
            [VMEM] + [VMEM] * 2,
            [square],
            64 * flops,
            marks, band, halo,
        )
        operands = (marks, band, sq_r, part_l, sums, more, twin)
        if step + 1 == STEPS:
            return call(
                last_kernel,
                jax.ShapeDtypeStruct((4, 4, S, S), BF),
                hbm,
                [SMEM] + [VMEM] * 7,
                [square, pltpu.VMEM((Q, 2 * Q), BF)]
                + [pltpu.VMEM((Q, 3 * Q), BF), pltpu.VMEM((4, 4, S, S), BF), pltpu.SemaphoreType.DMA((4,))],
                flops,
                table, *operands,
            )
        new, send, sq = call(
            step_kernel,
            [BANDED, SEND, jax.ShapeDtypeStruct((Q, 2 * Q), BF)],
            [VMEM] * 3,
            [VMEM] * 7,
            [square],
            flops,
            *operands,
        )
        band = call(
            step_left_kernel, BANDED, VMEM, [VMEM] * 5, [], 0, marks, band, sq, twin, new, alias={4: 0}
        )


def solution(mesh):
    return jax.shard_map(
        on_device,
        mesh=mesh,
        in_specs=(
            P("rows", None, None, None),
            P("rows", None, None, None),
            P("rows", None),
            P("rows", None),
        ),
        out_specs=P("rows", "rep", None, None),
        check_vma=False,
    )
```
